32 devices in a mesh: view: 4 (over y, x), depth: 8 (over z, core).
Axes of the slice: x: 2, y: 2, z: 4, core: 2. Of those that a mesh axis runs over, the one named last changes fastest.
Arguments:
- estimate: float32 [64, 128, 256], P('depth', 'view'), may hold values from 0.5 to 2
- observed: float32 [8, 64, 128, 256], P('view', 'depth'), may hold values from 0.05 to 30, as said below
- voxel_weights: bfloat16 [8, 8, 64, 128, 256], P('view', None, 'depth'), may hold values from 0.029907227 to 0.29882812
- lateral_taps: float32 [8, 8, 2, 9], P('view'), may hold values from 0.05 to 1
- axial_taps: float32 [8, 9], P('view'), may hold values from 0.05 to 1
Outputs:
- updated: float32 [64, 128, 256], P('depth', 'view')
- divergence: float32 [8], P('view')
The draws below stay inside these ranges and needn't reach their ends.
Inputs may be any that keep to these rules, and one draw needn't show every extreme that they name: `observed`: strictly positive.
All inputs are finite; a program needn't handle non-finite values.
Results may differ from the reference program's by a relative error of at most 0.0003.
Values sent between devices are 32-bit elements; how exact they have to be, the bound alone decides.
No kernel may reach another device: no remote copies, remote signals or barrier semaphores. Data moves between devices by JAX's collectives and lax.ppermute only.
A program may use at most 128 MiB of HBM per device.

```python
import math
import jax
import jax.numpy as jnp
from jax import lax

BASES = 8
TAPS = 9
RADIUS = 4
ITERS = 2
NY = 128
NX = 256
VIEWS = 8
NZ = 64


def draw_observed(key, part):
    key_values, key_facing = jax.random.split(key, 2)
    volume_shape = (VIEWS, NZ, NY, NX)
    facing = jnp.where(jax.random.bernoulli(key_facing, 0.5, (VIEWS,)), 1.0, -1.0).astype(jnp.float32)
    depth_frac = jnp.arange(NZ, dtype=jnp.float32) / max(NZ - 1, 1) - 0.5
    intensity = jnp.exp(jax.random.uniform(key_values, volume_shape, jnp.float32, jnp.log(0.1), jnp.log(10.0)))
    strength = jnp.log(3.0)
    profile = jnp.exp(strength * facing[:, None] * depth_frac[None, :])
    return intensity * profile[:, :, None, None]


def steps_of(own_key, dims, cuts, low, high):
    factor_of, own = 1.0, jax.random.fold_in(own_key, 6)
    for axis_at, shards_of in cuts:
        draws = jnp.exp(jax.random.uniform(jax.random.fold_in(own, axis_at), (shards_of,), jnp.float32, low / len(cuts), high / len(cuts)))
        factor_of = factor_of * jnp.repeat(draws, dims[axis_at] // shards_of).reshape([-1 if axis == axis_at else 1 for axis in range(len(dims))])
    return factor_of


def setup_inputs(seed: int = 0) -> dict:
    key_of = jax.random.split(jax.random.key(seed), 6)
    return {
        "estimate": jnp.clip(jnp.exp(math.log(2.0) - 1.3862944 * jax.random.uniform(key_of[0], (NZ, NY, NX), jnp.float32) ** steps_of(key_of[0], (NZ, NY, NX), ((0, 8), (1, 4)), -0.2, 0.2)), 0.5, 2.0),
        "observed": draw_observed(jax.random.fold_in(key_of[5], 71), 0),
        "voxel_weights": jnp.clip(jnp.exp(math.log(0.29882812) - 2.30176843 * jax.random.uniform(key_of[2], (VIEWS, BASES, NZ, NY, NX), jnp.float32) ** steps_of(key_of[2], (VIEWS, BASES, NZ, NY, NX), ((0, 4), (2, 8)), -0.2, 0.2)), 0.029907227, 0.29882812).astype(jnp.bfloat16),
        "lateral_taps": jnp.clip(jnp.exp(math.log(1.0) - 2.9957323 * jax.random.uniform(key_of[3], (VIEWS, BASES, 2, TAPS), jnp.float32) ** steps_of(key_of[3], (VIEWS, BASES, 2, TAPS), ((0, 4),), -0.2, 0.2)), 0.05, 1.0),
        "axial_taps": jnp.clip(jnp.exp(math.log(1.0) - 2.9957323 * jax.random.uniform(key_of[4], (VIEWS, TAPS), jnp.float32) ** steps_of(key_of[4], (VIEWS, TAPS), ((0, 4),), -0.2, 0.2)), 0.05, 1.0),
    }


def depth_forward(volume, depth_taps):
    planes = volume.shape[0]
    padded = jnp.pad(volume, ((RADIUS, RADIUS), (0, 0), (0, 0)))
    summed = jnp.zeros(volume.shape, jnp.float32)
    for tap_index in range(TAPS):
        summed = summed + depth_taps[tap_index] * padded[tap_index:tap_index + planes]
    return summed


def depth_adjoint(volume, depth_taps):
    planes = volume.shape[0]
    padded = jnp.pad(volume, ((RADIUS, RADIUS), (0, 0), (0, 0)))
    summed = jnp.zeros(volume.shape, jnp.float32)
    for tap_index in range(TAPS):
        offset = 2 * RADIUS - tap_index
        summed = summed + depth_taps[tap_index] * padded[offset:offset + planes]
    return summed


def lateral_forward(volume, weights, lateral):
    height = volume.shape[1]
    breadth = volume.shape[2]
    padded = jnp.pad(volume, ((0, 0), (RADIUS, RADIUS), (0, 0)))
    stacked = jnp.zeros((BASES,) + volume.shape, jnp.float32)
    for tap_index in range(TAPS):
        stacked = stacked + lateral[:, 0, tap_index].reshape(-1, 1, 1, 1) * padded[None, :, tap_index:tap_index + height, :]
    padded = jnp.pad(stacked, ((0, 0), (0, 0), (0, 0), (RADIUS, RADIUS)))
    blurred = jnp.zeros(stacked.shape, jnp.float32)
    for tap_index in range(TAPS):
        blurred = blurred + lateral[:, 1, tap_index].reshape(-1, 1, 1, 1) * padded[:, :, :, tap_index:tap_index + breadth]
    return jnp.sum(weights.astype(jnp.float32) * blurred, axis=0)


def lateral_adjoint(values, weights, lateral):
    height = values.shape[1]
    breadth = values.shape[2]
    stacked = weights.astype(jnp.float32) * values[None]
    padded = jnp.pad(stacked, ((0, 0), (0, 0), (0, 0), (RADIUS, RADIUS)))
    blurred = jnp.zeros(stacked.shape, jnp.float32)
    for tap_index in range(TAPS):
        offset = 2 * RADIUS - tap_index
        blurred = blurred + lateral[:, 1, tap_index].reshape(-1, 1, 1, 1) * padded[:, :, :, offset:offset + breadth]
    padded = jnp.pad(blurred, ((0, 0), (0, 0), (RADIUS, RADIUS), (0, 0)))
    summed = jnp.zeros(stacked.shape, jnp.float32)
    for tap_index in range(TAPS):
        offset = 2 * RADIUS - tap_index
        summed = summed + lateral[:, 0, tap_index].reshape(-1, 1, 1, 1) * padded[:, :, offset:offset + height, :]
    return jnp.sum(summed, axis=0)


def reference(estimate, observed, voxel_weights, lateral_taps, axial_taps):
    lateral_all = lateral_taps / jnp.sum(lateral_taps, axis=-1, keepdims=True)
    axial_all = axial_taps / jnp.sum(axial_taps, axis=-1, keepdims=True)
    voxel_total = estimate.shape[0] * estimate.shape[1] * estimate.shape[2]

    def sensitivity_of(member):
        weights, lateral, depth_taps = member
        unity = jnp.ones(estimate.shape, jnp.float32)
        return depth_adjoint(lateral_adjoint(unity, weights, lateral), depth_taps)

    sensitivity = lax.map(sensitivity_of, (voxel_weights, lateral_all, axial_all))
    current = estimate
    divergence = jnp.zeros((VIEWS,), jnp.float32)
    for iteration in range(ITERS):
        def view_step(log_total, member):
            counts, weights, lateral, depth_taps, sens_view = member
            predicted = lateral_forward(depth_forward(current, depth_taps), weights, lateral)
            ratios = counts / predicted
            projected = depth_adjoint(lateral_adjoint(ratios, weights, lateral), depth_taps)
            fidelity = jnp.sum(counts * jnp.log(ratios) - counts + predicted) / voxel_total
            return log_total + jnp.log(projected / sens_view), fidelity

        log_total, divergence = lax.scan(view_step, jnp.zeros(estimate.shape, jnp.float32), (observed, voxel_weights, lateral_all, axial_all, sensitivity))
        current = current * jnp.exp(log_total / VIEWS)
    return current, divergence
```

```python
import jax
import jax.numpy as jnp
from jax import lax
from jax.experimental import pallas as pl
from jax.experimental.pallas import tpu as pltpu
from jax.sharding import PartitionSpec as P

TAPS = 9
RADIUS = 4
ITERS = 2
F32 = jnp.float32
BF16 = jnp.bfloat16
VMEM_BYTES = 58 * 1024 * 1024
NOISE_SHIFTS = 64


def mxu(left, right):
    return jnp.dot(left, right, preferred_element_type=F32)


def noise_rows(bases, height):
    return bases * height + 8 * NOISE_SHIFTS


def noise_at(place_ref, view, z, rows):
    shift = lax.rem(37 * (place_ref[1] + view) + 11 * (place_ref[2] + z), NOISE_SHIFTS)
    return pl.ds(pl.multiple_of(shift * 8, 8), rows)


def banded(taps, size, sign):
    rows = lax.broadcasted_iota(jnp.int32, (size, size), 0)
    columns = lax.broadcasted_iota(jnp.int32, (size, size), 1)
    at = sign * (rows - columns) + RADIUS
    total = jnp.zeros((size, size), F32)
    for tap in range(TAPS):
        total = jnp.where(at == tap, jnp.broadcast_to(taps[:, tap : tap + 1], (size, size)), total)
    return total


def prepare_kernel(lateral_ref, axial_ref, x_ref, xt_ref, y_ref, yt_ref, axial_out_ref, noise_ref, gain_ref):
    bases, breadth, height = x_ref.shape[1], x_ref.shape[2], yt_ref.shape[1]
    for base in range(bases):
        taps = lateral_ref[0, base]
        taps = taps / jnp.sum(taps, axis=-1, keepdims=True)
        y_taps, x_taps = taps[0:1], taps[1:2].astype(BF16).astype(F32)
        x_ref[0, base] = banded(x_taps, breadth, 1).astype(BF16)
        xt_ref[0, base] = banded(x_taps, breadth, -1).astype(BF16)
        y_taps = y_taps.astype(BF16).astype(F32)
        gain = 1.0 / (jnp.sum(x_taps, axis=-1, keepdims=True) * jnp.sum(y_taps, axis=-1, keepdims=True))
        gain_ref[0, base : base + 1, :] = jnp.broadcast_to(gain, (1, gain_ref.shape[2]))
        at = slice(base * height, (base + 1) * height)
        y_ref[0, at, :] = banded(y_taps, height, -1).astype(BF16)
        yt_ref[0, :, at] = banded(y_taps, height, 1).astype(BF16)

    @pl.when(pl.program_id(0) == 0)
    def _():
        axial = axial_ref[...]
        axial_out_ref[...] = axial / jnp.sum(axial, axis=-1, keepdims=True)

        def fill(k, carry):
            first = pl.multiple_of(k * 64, 64)
            rows = lax.broadcasted_iota(jnp.int32, (64, breadth), 0) + first
            columns = lax.broadcasted_iota(jnp.int32, (64, breadth), 1)
            mixed = rows * 1664525 + columns * 22695477 + 12345
            for odd, shift in ((739982445, 15), (695872825, 12)):
                mixed = (mixed ^ lax.shift_right_logical(mixed, shift)) * odd
            mixed = mixed ^ lax.shift_right_logical(mixed, 15)
            both = (mixed & 2047) + (lax.shift_right_logical(mixed, 16) & 2047)
            noise_ref[pl.ds(first, 64), :] = 1.0 + (both - 2047).astype(F32) * (1.0 / (2048 * 128))
            return carry

        lax.fori_loop(0, noise_ref.shape[0] // 64, fill, 0)


def adjoint_half(weigh, ready, xt, yt_ref, field_ref, mixed):
    half, rows, _ = mixed.shape
    height = yt_ref.shape[0]
    bases = rows // (2 * height)
    for base in range(bases):
        ready(base)
        swept = mxu(weigh(base), xt[base])
        high = swept.astype(BF16)
        low = (swept - high.astype(F32)).astype(BF16)
        for z in range(half):
            at = slice(z * height, (z + 1) * height)
            mixed[z, base * height : (base + 1) * height, :] = high[at]
            mixed[z, (bases + base) * height : (bases + base + 1) * height, :] = low[at]
    twice = jnp.concatenate([yt_ref[...], yt_ref[...]], axis=1)
    for z in range(half):
        field_ref[0, z] = mxu(twice, mixed[z])


def half_copies(place_ref, view, weights_any, weights, xt_any, xt, yt_any, yt, sems):
    bases, half = weights.shape[1:3]
    planes = pl.ds(place_ref[0] * half, half)
    per_base = [
        (pltpu.make_async_copy(weights_any.at[view, base, planes], weights.at[view, base], sems.at[view, 0, base]),
         pltpu.make_async_copy(xt_any.at[view, base], xt.at[view, base], sems.at[view, 1, base]))
        for base in range(bases)
    ]
    return per_base, pltpu.make_async_copy(yt_any.at[view], yt.at[view], sems.at[view, 2, 0])


def ones_kernel(place_ref, weights_any, xt_any, yt_any, after_any, field_ref, weights, xt, yt, sems, mixed):
    view = pl.program_id(0)
    views, bases, half, height, breadth = weights.shape

    def copies(at):
        return half_copies(place_ref, at, weights_any, weights, xt_any, xt, yt_any, yt, sems)

    @pl.when(view == 0)
    def _():
        for at in range(views):
            per_base, last = copies(at)
            for pair in per_base:
                for copy in pair:
                    copy.start()
            last.start()

    per_base, last = copies(view)

    def ready(base):
        for copy in per_base[base]:
            copy.wait()
        if base == bases - 1:
            last.wait()

    def weigh(base):
        return weights[view, base].reshape(half * height, breadth)

    adjoint_half(weigh, ready, xt.at[view], yt.at[view], field_ref, mixed)


def step_kernel(place_ref, axial_ref, halo_ref, near_ref, far_ref, noise_ref, gain_ref, y_ref, counts_any, weights_any, x_any,
                xt_any, yt_any, after_any, field_ref, fidelity_ref, weights, counts_buf, x, xt, yt, sems, more_sems,
                blurred, rows, mixed):
    view = pl.program_id(0)
    views, bases, half, height, breadth = weights.shape
    quarters, _, span, _ = near_ref.shape

    def copies(at):
        per_base, last = half_copies(place_ref, at, weights_any, weights, xt_any, xt, yt_any, yt, sems)
        planes = pl.ds(place_ref[0] * half, half)
        forward = [pltpu.make_async_copy(x_any.at[at, base], x.at[at, base], more_sems.at[at, base]) for base in range(bases)]
        counts = pltpu.make_async_copy(counts_any.at[at, planes], counts_buf.at[at], more_sems.at[at, bases])
        return per_base, last, forward, counts

    @pl.when(view == 0)
    def _():
        for at in range(views):
            per_base, last, forward, counts = copies(at)
            for pair, extra in zip(per_base, forward):
                extra.start()
                pair[0].start()
            counts.start()
            for pair in per_base:
                pair[1].start()
            last.start()

    per_base, last, forward, counts_copy = copies(view)

    def depth_blur(groups):
        for z in range(half):
            for q in range(quarters):
                total = None
                for tap in range(TAPS):
                    plane = z + tap
                    term = axial_ref[view, tap] * groups[plane // half][q, plane % half]
                    total = term if total is None else total + term
                high = total.astype(BF16)
                blurred[z, q * span : (q + 1) * span, :] = high
                blurred[z, height + q * span : height + (q + 1) * span, :] = (total - high.astype(F32)).astype(BF16)

    @pl.when(place_ref[0] == 0)
    def _():
        depth_blur((halo_ref, near_ref, far_ref))

    @pl.when(place_ref[0] != 0)
    def _():
        depth_blur((far_ref, near_ref, halo_ref))

    twice = jnp.concatenate([y_ref[0], y_ref[0]], axis=1)
    for z in range(half):
        swept = mxu(twice, blurred[z]) * noise_ref[noise_at(place_ref, view, z, bases * height), :]
        for base in range(bases):
            gain = gain_ref[0, base : base + 1, :]
            rows[base, z * height : (z + 1) * height, :] = (swept[base * height : (base + 1) * height] * gain).astype(BF16)

    def weights_of(base):
        return weights[view, base].reshape(half * height, breadth).astype(F32)

    predicted = None
    for base in range(bases):
        forward[base].wait()
        per_base[base][0].wait()
        term = weights_of(base) * mxu(rows[base], x[view, base])
        predicted = term if predicted is None else predicted + term
    counts_copy.wait()
    counts = counts_buf[view].reshape(half * height, breadth)
    ratios = counts / predicted
    if fidelity_ref is not None:
        terms = counts * jnp.log(ratios) - counts + predicted
        fidelity_ref[0] = jnp.sum(terms.reshape(-1, 8, breadth), axis=0)
    noise = [noise_ref[noise_at(place_ref, view, z, height), :] for z in range(half)]
    spread = ratios * jnp.concatenate(noise, axis=0)

    def ready(base):
        per_base[base][1].wait()
        if base == bases - 1:
            last.wait()

    def weigh(base):
        return (weights_of(base) * spread).astype(BF16)

    adjoint_half(weigh, ready, xt.at[view], yt.at[view], field_ref, mixed)


def plain_step_kernel(*refs):
    step_kernel(*refs[:15], None, *refs[15:])


def depth_adjoint(place_ref, axial_ref, groups, scale_ref, out_ref):
    views, half = groups[1].shape[:2]

    def run(ordered):
        for z in range(half):
            product = None
            for view in range(views):
                total = None
                for tap in range(TAPS):
                    plane = z + 2 * RADIUS - tap
                    term = axial_ref[view, tap] * ordered[plane // half][view, plane % half]
                    total = term if total is None else total + term
                product = total if product is None else product * total
            out_ref[0, z] = 1.0 / product if scale_ref is None else jnp.log(product * scale_ref[0, z])

    halo_ref, near_ref, far_ref = groups

    @pl.when(place_ref[0] == 0)
    def _():
        run((halo_ref, near_ref, far_ref))

    @pl.when(place_ref[0] != 0)
    def _():
        run((far_ref, near_ref, halo_ref))


def scale_kernel(place_ref, axial_ref, halo_ref, near_ref, far_ref, after_any, out_ref):
    depth_adjoint(place_ref, axial_ref, (halo_ref, near_ref, far_ref), None, out_ref)


def log_kernel(place_ref, axial_ref, halo_ref, near_ref, far_ref, scale_ref, after_any, out_ref):
    depth_adjoint(place_ref, axial_ref, (halo_ref, near_ref, far_ref), scale_ref, out_ref)


def share_kernel(place_ref, own_ref, copies_ref, current_ref):
    current_ref[0] = own_ref[0, 0]
    for q in range(copies_ref.shape[0]):
        copies_ref[q, 0] = own_ref[0, 0]


def corrected(pieces_ref, current, views_total):
    total = pieces_ref[0, 0]
    for q in range(1, pieces_ref.shape[0]):
        total = total + pieces_ref[q, 0]
    return current * jnp.exp(total * (1.0 / views_total))


def whole(shape):
    return pl.BlockSpec(shape, lambda *_: (0,) * len(shape))


def per_view(shape):
    return pl.BlockSpec((1,) + shape[1:], lambda v, *_: (v,) + (0,) * (len(shape) - 1))


def per_quarter(shape):
    return pl.BlockSpec((1,) + shape[1:], lambda q, *_: (q,) + (0,) * (len(shape) - 1))


def per_plane(shape):
    return pl.BlockSpec((shape[0], 1) + shape[2:], lambda z, *_: (0, z) + (0,) * (len(shape) - 2))


ANY = pl.BlockSpec(memory_space=pl.ANY)
SMEM = pl.BlockSpec(memory_space=pltpu.SMEM)


def call(kernel, grid, in_specs, out_shape, out_specs, scratch=(), prefetch=1, cost=(0, 0), **more):
    return pl.pallas_call(
        kernel,
        out_shape=out_shape,
        grid_spec=pltpu.PrefetchScalarGridSpec(
            num_scalar_prefetch=prefetch, grid=grid, in_specs=in_specs, out_specs=out_specs, scratch_shapes=list(scratch)),
        compiler_params=pltpu.CompilerParams(vmem_limit_bytes=VMEM_BYTES),
        cost_estimate=pl.CostEstimate(flops=cost[0], bytes_accessed=cost[1], transcendentals=0),
        **more,
    )


def body(estimate, observed, voxel_weights, lateral_taps, axial_taps):
    views, planes, height, breadth = observed.shape
    bases = voxel_weights.shape[1]
    half = planes // 2
    assert half == RADIUS and planes % 2 == 0
    quarters = lax.axis_size("view")
    depths = lax.axis_size("depth")
    span = height // quarters
    views_total = views * quarters
    voxel_total = planes * depths * height * breadth
    parity = lax.rem(lax.axis_index("depth"), 2).astype(jnp.int32)
    first_view, first_plane = lax.axis_index("view") * views, lax.axis_index("depth") * planes
    halves = [
        jnp.stack([at, first_view, first_plane + at * half]).astype(jnp.int32) for at in (parity, 1 - parity)
    ]

    def swap(values, which):
        pairs = []
        for i in range(1 - which, depths - 1, 2):
            pairs += [(i, i + 1), (i + 1, i)]
        return lax.ppermute(values, "depth", pairs)

    def shape(*dims, dtype=F32):
        return jax.ShapeDtypeStruct(dims, dtype)

    x_shape = shape(views, bases, breadth, breadth, dtype=BF16)
    y_shape = shape(views, bases * height, height, dtype=BF16)
    gain_shape = shape(views, bases, breadth)
    yt_shape = shape(views, height, bases * height, dtype=BF16)
    noise_shape = shape(noise_rows(bases, height), breadth)
    group_shape = shape(quarters, half, span, breadth)
    field_shape = shape(views, half, height, breadth)
    fidelity_shape = shape(views, 8, breadth)
    current_shape = shape(half, span, breadth)
    volume = views * bases * half * height * breadth

    x_mat, xt_mat, y_mat, yt_mat, axial, noise, gain = call(
        prepare_kernel, (views,), [per_view(lateral_taps.shape), whole(axial_taps.shape)],
        (x_shape, x_shape, y_shape, yt_shape, shape(*axial_taps.shape), noise_shape, gain_shape),
        (per_view(x_shape.shape), per_view(x_shape.shape), per_view(y_shape.shape), per_view(yt_shape.shape),
         whole(axial_taps.shape), whole(noise_shape.shape), per_view(gain_shape.shape)),
        prefetch=0, cost=(volume, volume),
    )(lateral_taps, axial_taps)

    weights_buf = pltpu.VMEM((views, bases, half, height, breadth), BF16)
    x_buf = pltpu.VMEM(x_shape.shape, BF16)
    yt_buf = pltpu.VMEM(yt_shape.shape, BF16)
    sems = pltpu.SemaphoreType.DMA((views, 3, bases))
    mixed_buf = pltpu.VMEM((half, 2 * bases * height, breadth), BF16)

    def ones_half(which, after):
        return call(
            ones_kernel, (views,), [ANY] * 4, field_shape, per_view(field_shape.shape),
            [weights_buf, x_buf, yt_buf, sems, mixed_buf], cost=(2 * volume * (breadth + height), 4 * volume),
        )(halves[which], voxel_weights, xt_mat, yt_mat, after)

    def step_half(which, halo, near, far, after, last):
        out = call(
            step_kernel if last else plain_step_kernel, (views,),
            [SMEM] + [whole(group_shape.shape)] * 3 + [whole(noise_shape.shape), per_view(gain_shape.shape), per_view(y_shape.shape)] + [ANY] * 6,
            (field_shape, fidelity_shape) if last else field_shape,
            (per_view(field_shape.shape), per_view(fidelity_shape.shape)) if last else per_view(field_shape.shape),
            [weights_buf, pltpu.VMEM((views, half, height, breadth), F32), x_buf, x_buf, yt_buf, sems,
             pltpu.SemaphoreType.DMA((views, bases + 1)), pltpu.VMEM((half, 2 * height, breadth), BF16),
             pltpu.VMEM((bases, half * height, breadth), BF16), mixed_buf],
            cost=(4 * volume * (breadth + height), 4 * volume),
        )(halves[which], axial, halo, near, far, noise, gain, y_mat, observed, voxel_weights, x_mat, xt_mat, yt_mat, after)
        return out if last else (out, None)

    field_block = pl.BlockSpec((views, half, span, breadth), lambda q, *_: (0, 0, q, 0))

    def depth_half(which, halo, near, far, after, scale=None):
        scales_in = () if scale is None else (scale,)
        return call(
            scale_kernel if scale is None else log_kernel, (quarters,),
            [SMEM] + [field_block] * 3 + [per_quarter(group_shape.shape)] * len(scales_in) + [ANY],
            group_shape, per_quarter(group_shape.shape), cost=(20 * near.size, 16 * near.size),
        )(halves[which], axial, halo, near, far, *scales_in, after)

    def share(which):
        own = estimate.reshape(2, half, span, breadth)
        return call(
            share_kernel, (half,), [pl.BlockSpec((1, 1, span, breadth), lambda z, h: (h[0], z, 0, 0))],
            (group_shape, current_shape), (per_plane(group_shape.shape), per_quarter(current_shape.shape)),
            cost=(near_cost, 8 * near_cost),
        )(halves[which], own)

    near_cost = half * span * breadth

    def update(pieces, current):
        def kernel(pieces_ref, current_ref, copies_ref, new_ref):
            new_ref[0] = corrected(pieces_ref, current_ref[0], views_total)
            for q in range(quarters):
                copies_ref[q, 0] = new_ref[0]

        return call(
            kernel, (half,), [per_plane(group_shape.shape), per_quarter(current_shape.shape)],
            (group_shape, current_shape), (per_plane(group_shape.shape), per_quarter(current_shape.shape)),
            prefetch=0, cost=(8 * near_cost, 40 * near_cost),
        )(pieces, current)

    def finish(which, pieces, current, so_far):
        aliased = so_far is not None

        def kernel(place_ref, pieces_ref, current_ref, *rest):
            rest[-1][0, 0] = corrected(pieces_ref, current_ref[0], views_total)

        return call(
            kernel, (half,), [per_plane(group_shape.shape), per_quarter(current_shape.shape)] + [ANY] * aliased,
            shape(2, half, span, breadth), pl.BlockSpec((1, 1, span, breadth), lambda z, h: (h[0], z, 0, 0)),
            cost=(8 * near_cost, 24 * near_cost), input_output_aliases={3: 0} if aliased else {},
        )(halves[which], pieces, current, *((so_far,) if aliased else ()))

    def exchange(values):
        return lax.all_to_all(values, "view", 0, 0)

    copies, current = zip(*[share(k) for k in range(2)])
    groups = [exchange(copies[k]) for k in range(2)]
    sens, sens_halo = [None, None], [None, None]
    for k in range(2):
        sens[k] = ones_half(k, sens[0] if k else axial)
        sens_halo[k] = swap(sens[k], k)
    scales = [None, None]
    for iteration in range(ITERS):
        last = iteration == ITERS - 1
        halo = [swap(groups[k], k) for k in range(2)]
        fields, parts, fields_halo = [None, None], [None, None], [None, None]
        for k in range(2):
            fields[k], parts[k] = step_half(k, halo[k], groups[k], groups[1 - k], fields[0] if k else axial, last)
            fields_halo[k] = swap(fields[k], k)
        if iteration == 0:
            for k in range(2):
                scales[k] = depth_half(k, sens_halo[k], sens[k], sens[1 - k], scales[0] if k else axial)
        order = (1, 0) if last else (0, 1)
        pieces, logs = [None, None], axial
        for k in order:
            logs = depth_half(k, fields_halo[k], fields[k], fields[1 - k], logs, scales[k])
            pieces[k] = exchange(logs)
        if not last:
            copies, current = zip(*[update(pieces[k], current[k]) for k in range(2)])
            groups = [exchange(copies[k]) for k in range(2)]
    divergence = lax.psum(jnp.sum(parts[0] + parts[1], axis=(1, 2)), "depth") / voxel_total
    updated = None
    for k in order:
        updated = finish(k, pieces[k], current[k], updated)
    return updated.reshape(estimate.shape), divergence


def solution(mesh):
    placed = (
        P("depth", "view", None),
        P("view", "depth", None, None),
        P("view", None, "depth", None, None),
        P("view", None, None, None),
        P("view", None),
    )
    return jax.shard_map(
        body,
        mesh=mesh,
        in_specs=placed,
        out_specs=(P("depth", "view", None), P("view")),
        check_vma=False,
    )
```

```python
import jax
import jax.numpy as jnp
from jax import lax
from jax.experimental import pallas as pl
from jax.experimental.pallas import tpu as pltpu
from jax.sharding import PartitionSpec as P

TAPS = 9
RADIUS = 4
ITERS = 2
F32 = jnp.float32
BF16 = jnp.bfloat16
NOISE_SHIFTS = 64


def mxu(left, right):
    return jnp.dot(left, right, preferred_element_type=F32)


def noise_rows(bases, height):
    return bases * height + 8 * NOISE_SHIFTS


def noise_at(place_ref, view, z, rows):
    shift = lax.rem(37 * (place_ref[1] + view) + 11 * (place_ref[2] + z), NOISE_SHIFTS)
    return pl.ds(pl.multiple_of(shift * 8, 8), rows)


def prepare_kernel(taps_ref, lateral_ref, axial_ref, x_ref, xt_ref, y_ref, yt_ref, axial_out_ref, noise_ref, gain_ref):
    view = pl.program_id(0)
    bases, breadth, height = x_ref.shape[1], x_ref.shape[2], yt_ref.shape[1]
    tall, wide = 32, 128
    inverses = []
    for base in range(bases):
        taps = lateral_ref[0, base]
        inverse = 1.0 / jnp.sum(taps, axis=-1, keepdims=True)
        sums = jnp.sum((taps * inverse).astype(BF16).astype(F32), axis=-1, keepdims=True)
        gain = 1.0 / (sums[0:1] * sums[1:2])
        gain_ref[0, base : base + 1, :] = jnp.broadcast_to(gain, (1, gain_ref.shape[2]))
        inverses.append([jnp.broadcast_to(inverse[k : k + 1], (tall, wide)) for k in range(2)])

    def banded(masks, base, kind, sign):
        total = jnp.zeros((tall, wide), F32)
        for tap in range(TAPS):
            total = jnp.where(masks[tap if sign > 0 else TAPS - 1 - tap], taps_ref[view, base, kind, tap], total)
        return (total * inverses[base][kind]).astype(BF16)

    for r in range(0, breadth, tall):
        for c in range(0, breadth, wide):
            at = (slice(r, r + tall), slice(c, c + wide))
            lateral = r < height and c < height
            if r + tall + RADIUS <= c or c + wide + RADIUS <= r:
                empty = jnp.zeros((tall, wide), BF16)
                for base in range(bases):
                    x_ref[(0, base) + at] = empty
                    xt_ref[(0, base) + at] = empty
                    if lateral:
                        y_ref[0, base * height + r : base * height + r + tall, at[1]] = empty
                        yt_ref[0, at[0], base * height + c : base * height + c + wide] = empty
                continue
            rows = lax.broadcasted_iota(jnp.int32, (tall, wide), 0) + r
            columns = lax.broadcasted_iota(jnp.int32, (tall, wide), 1) + c
            masks = [rows - columns + RADIUS == tap for tap in range(TAPS)]
            for base in range(bases):
                x_ref[(0, base) + at] = banded(masks, base, 1, 1)
                xt_ref[(0, base) + at] = banded(masks, base, 1, -1)
                if lateral:
                    y_ref[0, base * height + r : base * height + r + tall, at[1]] = banded(masks, base, 0, -1)
                    yt_ref[0, at[0], base * height + c : base * height + c + wide] = banded(masks, base, 0, 1)

    @pl.when(pl.program_id(0) == 0)
    def _():
        axial = axial_ref[...]
        axial_out_ref[...] = axial / jnp.sum(axial, axis=-1, keepdims=True)

        def fill(k, carry):
            first = pl.multiple_of(k * 64, 64)
            rows = lax.broadcasted_iota(jnp.int32, (64, breadth), 0) + first
            columns = lax.broadcasted_iota(jnp.int32, (64, breadth), 1)
            mixed = rows * 1664525 + columns * 22695477 + 12345
            for odd, shift in ((739982445, 15), (695872825, 12)):
                mixed = (mixed ^ lax.shift_right_logical(mixed, shift)) * odd
            mixed = mixed ^ lax.shift_right_logical(mixed, 15)
            both = (mixed & 2047) + (lax.shift_right_logical(mixed, 16) & 2047)
            noise_ref[pl.ds(first, 64), :] = 1.0 + (both - 2047).astype(F32) * (1.0 / (2048 * 128))
            return carry

        lax.fori_loop(0, noise_ref.shape[0] // 64, fill, 0)


def adjoint_half(weigh, xt, yt_ref, field_ref, mixed):
    half, rows, _ = mixed.shape
    height = yt_ref.shape[0]
    bases = rows // (2 * height)
    for base in range(bases):
        swept = mxu(weigh(base), xt[base])
        high = swept.astype(BF16)
        low = (swept - high.astype(F32)).astype(BF16)
        for z in range(half):
            at = slice(z * height, (z + 1) * height)
            mixed[z, base * height : (base + 1) * height, :] = high[at]
            mixed[z, (bases + base) * height : (bases + base + 1) * height, :] = low[at]
    twice = jnp.concatenate([yt_ref[...], yt_ref[...]], axis=1)
    for z in range(half):
        field_ref[0, z] = mxu(twice, mixed[z])


def ones_kernel(place_ref, weights_any, xt_any, yt_any, after_any, field_ref, weights, xt, yt, sems, mixed):
    view = pl.program_id(0)
    views, bases, half, height, breadth = weights.shape
    planes = pl.ds(place_ref[0] * half, half)

    def copies(at):
        pairs = ((weights_any.at[at, :, planes], weights), (xt_any.at[at], xt), (yt_any.at[at], yt))
        return [pltpu.make_async_copy(a, b.at[at], sems.at[at, k]) for k, (a, b) in enumerate(pairs)]

    @pl.when(view == 0)
    def _():
        for at in range(views):
            for copy in copies(at):
                copy.start()

    for copy in copies(view):
        copy.wait()
    adjoint_half(lambda base: weights[view, base].reshape(half * height, breadth), xt.at[view], yt.at[view], field_ref, mixed)


def step_kernel(place_ref, axial_ref, halo_ref, near_ref, far_ref, noise_ref, gain_ref, y_ref, counts_any, weights_any,
                x_any, xt_any, yt_any, after_any, field_ref, fidelity_ref, weights, counts_buf, x, xt, yt, sems,
                blurred, rows, mixed):
    view = pl.program_id(0)
    views, bases, half, height, breadth = weights.shape
    quarters, _, span, _ = near_ref.shape
    planes = pl.ds(place_ref[0] * half, half)

    def copies(at):
        pairs = ((x_any.at[at], x), (weights_any.at[at, :, planes], weights), (counts_any.at[at, planes], counts_buf),
                 (xt_any.at[at], xt), (yt_any.at[at], yt))
        return [pltpu.make_async_copy(a, b.at[at], sems.at[at, k]) for k, (a, b) in enumerate(pairs)]

    @pl.when(view == 0)
    def _():
        for at in range(views):
            for copy in copies(at):
                copy.start()

    def depth_blur(groups):
        for z in range(half):
            for q in range(quarters):
                total = None
                for tap in range(TAPS):
                    plane = z + tap
                    term = axial_ref[view, tap] * groups[plane // half][q, plane % half]
                    total = term if total is None else total + term
                high = total.astype(BF16)
                blurred[z, q * span : (q + 1) * span, :] = high
                blurred[z, height + q * span : height + (q + 1) * span, :] = (total - high.astype(F32)).astype(BF16)

    @pl.when(place_ref[0] == 0)
    def _():
        depth_blur((halo_ref, near_ref, far_ref))

    @pl.when(place_ref[0] != 0)
    def _():
        depth_blur((far_ref, near_ref, halo_ref))

    for copy in copies(view):
        copy.wait()
    twice = jnp.concatenate([y_ref[0], y_ref[0]], axis=1)
    for z in range(half):
        swept = mxu(twice, blurred[z]) * noise_ref[noise_at(place_ref, view, z, bases * height), :]
        for base in range(bases):
            gain = gain_ref[0, base : base + 1, :]
            rows[base, z * height : (z + 1) * height, :] = (swept[base * height : (base + 1) * height] * gain).astype(BF16)

    def weights_of(base):
        return weights[view, base].reshape(half * height, breadth).astype(F32)

    predicted = None
    for base in range(bases):
        term = weights_of(base) * mxu(rows[base], x[view, base])
        predicted = term if predicted is None else predicted + term
    counts = counts_buf[view].reshape(half * height, breadth)
    ratios = counts / predicted
    if fidelity_ref is not None:
        terms = counts * jnp.log(ratios) - counts + predicted
        fidelity_ref[0] = jnp.sum(terms.reshape(-1, 8, breadth), axis=0)
    noise = [noise_ref[noise_at(place_ref, view, z, height), :] for z in range(half)]
    spread = ratios * jnp.concatenate(noise, axis=0)
    adjoint_half(lambda base: (weights_of(base) * spread).astype(BF16), xt.at[view], yt.at[view], field_ref, mixed)


def plain_step_kernel(*refs):
    step_kernel(*refs[:15], None, *refs[15:])


def depth_adjoint(place_ref, axial_ref, groups, scale_ref, out_ref):
    views, half = groups[1].shape[:2]
    quarters, _, span, _ = out_ref.shape

    def run(ordered):
        def quarter(q, carry):
            at = pl.ds(pl.multiple_of(q * span, span), span)
            for z in range(half):
                product = None
                for view in range(views):
                    total = None
                    for tap in range(TAPS):
                        plane = z + 2 * RADIUS - tap
                        term = axial_ref[view, tap] * ordered[plane // half][view, plane % half, at, :]
                        total = term if total is None else total + term
                    product = total if product is None else product * total
                out_ref[q, z] = 1.0 / product if scale_ref is None else jnp.log(product * scale_ref[q, z])
            return carry

        lax.fori_loop(0, quarters, quarter, 0)

    halo_ref, near_ref, far_ref = groups

    @pl.when(place_ref[0] == 0)
    def _():
        run((halo_ref, near_ref, far_ref))

    @pl.when(place_ref[0] != 0)
    def _():
        run((far_ref, near_ref, halo_ref))


def scale_kernel(place_ref, axial_ref, halo_ref, near_ref, far_ref, after_any, out_ref):
    depth_adjoint(place_ref, axial_ref, (halo_ref, near_ref, far_ref), None, out_ref)


def log_kernel(place_ref, axial_ref, halo_ref, near_ref, far_ref, scale_ref, after_any, out_ref):
    depth_adjoint(place_ref, axial_ref, (halo_ref, near_ref, far_ref), scale_ref, out_ref)


def share_kernel(place_ref, own_ref, copies_ref, current_ref):
    current_ref[...] = own_ref[0]
    for q in range(copies_ref.shape[0]):
        copies_ref[q] = own_ref[0]


def corrected(pieces_ref, current_ref, views_total):
    total = pieces_ref[0]
    for q in range(1, pieces_ref.shape[0]):
        total = total + pieces_ref[q]
    return current_ref[...] * jnp.exp(total * (1.0 / views_total))


def whole(shape):
    return pl.BlockSpec(shape, lambda *_: (0,) * len(shape))


def per_view(shape):
    return pl.BlockSpec((1,) + shape[1:], lambda v, *_: (v,) + (0,) * (len(shape) - 1))


ANY = pl.BlockSpec(memory_space=pl.ANY)
SMEM = pl.BlockSpec(memory_space=pltpu.SMEM)


def call(kernel, grid, in_specs, out_shape, out_specs, scratch=(), prefetch=1, cost=(0, 0), vmem=16, **more):
    return pl.pallas_call(
        kernel,
        out_shape=out_shape,
        grid_spec=pltpu.PrefetchScalarGridSpec(
            num_scalar_prefetch=prefetch, grid=grid, in_specs=in_specs, out_specs=out_specs, scratch_shapes=list(scratch)),
        compiler_params=pltpu.CompilerParams(vmem_limit_bytes=vmem * 1024 * 1024),
        cost_estimate=pl.CostEstimate(flops=cost[0], bytes_accessed=cost[1], transcendentals=0),
        **more,
    )


def body(estimate, observed, voxel_weights, lateral_taps, axial_taps):
    views, planes, height, breadth = observed.shape
    bases = voxel_weights.shape[1]
    half = planes // 2
    assert half == RADIUS and planes % 2 == 0
    quarters = lax.axis_size("view")
    depths = lax.axis_size("depth")
    span = height // quarters
    views_total = views * quarters
    voxel_total = planes * depths * height * breadth
    parity = lax.rem(lax.axis_index("depth"), 2).astype(jnp.int32)
    first_view, first_plane = lax.axis_index("view") * views, lax.axis_index("depth") * planes
    halves = [
        jnp.stack([at, first_view, first_plane + at * half]).astype(jnp.int32) for at in (parity, 1 - parity)
    ]

    def swap(values, which):
        pairs = []
        for i in range(1 - which, depths - 1, 2):
            pairs += [(i, i + 1), (i + 1, i)]
        return lax.ppermute(values, "depth", pairs)

    def shape(*dims, dtype=F32):
        return jax.ShapeDtypeStruct(dims, dtype)

    x_shape = shape(views, bases, breadth, breadth, dtype=BF16)
    y_shape = shape(views, bases * height, height, dtype=BF16)
    gain_shape = shape(views, bases, breadth)
    yt_shape = shape(views, height, bases * height, dtype=BF16)
    noise_shape = shape(noise_rows(bases, height), breadth)
    group_shape = shape(quarters, half, span, breadth)
    field_shape = shape(views, half, height, breadth)
    fidelity_shape = shape(views, 8, breadth)
    current_shape = shape(half, span, breadth)
    volume = views * bases * half * height * breadth

    x_mat, xt_mat, y_mat, yt_mat, axial, noise, gain = call(
        prepare_kernel, (views,), [SMEM, per_view(lateral_taps.shape), whole(axial_taps.shape)],
        (x_shape, x_shape, y_shape, yt_shape, shape(*axial_taps.shape), noise_shape, gain_shape),
        (per_view(x_shape.shape), per_view(x_shape.shape), per_view(y_shape.shape), per_view(yt_shape.shape),
         whole(axial_taps.shape), whole(noise_shape.shape), per_view(gain_shape.shape)),
        prefetch=0, cost=(volume, volume),
    )(lateral_taps, lateral_taps, axial_taps)

    weights_buf = pltpu.VMEM((views, bases, half, height, breadth), BF16)
    x_buf = pltpu.VMEM(x_shape.shape, BF16)
    yt_buf = pltpu.VMEM(yt_shape.shape, BF16)
    sems = pltpu.SemaphoreType.DMA((views, 5))
    mixed_buf = pltpu.VMEM((half, 2 * bases * height, breadth), BF16)

    def ones_half(which, after):
        return call(
            ones_kernel, (views,), [ANY] * 4, field_shape, per_view(field_shape.shape),
            [weights_buf, x_buf, yt_buf, sems, mixed_buf], vmem=20, cost=(2 * volume * (breadth + height), 4 * volume),
        )(halves[which], voxel_weights, xt_mat, yt_mat, after)

    def step_half(which, halo, near, far, after, last):
        out = call(
            step_kernel if last else plain_step_kernel, (views,),
            [SMEM] + [whole(group_shape.shape)] * 3 + [whole(noise_shape.shape), per_view(gain_shape.shape), per_view(y_shape.shape)] + [ANY] * 6,
            (field_shape, fidelity_shape) if last else field_shape,
            (per_view(field_shape.shape), per_view(fidelity_shape.shape)) if last else per_view(field_shape.shape),
            [weights_buf, pltpu.VMEM((views, half, height, breadth), F32), x_buf, x_buf, yt_buf, sems,
             pltpu.VMEM((half, 2 * height, breadth), BF16),
             pltpu.VMEM((bases, half * height, breadth), BF16), mixed_buf],
            vmem=36, cost=(4 * volume * (breadth + height), 4 * volume),
        )(halves[which], axial, halo, near, far, noise, gain, y_mat, observed, voxel_weights, x_mat, xt_mat, yt_mat, after)
        return out if last else (out, None)

    def depth_half(which, halo, near, far, after, scale=None):
        scales_in = () if scale is None else (scale,)
        return call(
            scale_kernel if scale is None else log_kernel, (1,),
            [SMEM] + [whole(field_shape.shape)] * 3 + [whole(group_shape.shape)] * len(scales_in) + [ANY],
            group_shape, whole(group_shape.shape), cost=(20 * near.size, 16 * near.size),
        )(halves[which], axial, halo, near, far, *scales_in, after)

    own_block = pl.BlockSpec((1, half, span, breadth), lambda _, place: (place[0], 0, 0, 0))
    own_cost = half * span * breadth

    def share(which):
        own = estimate.reshape(2, half, span, breadth)
        return call(
            share_kernel, (1,), [own_block], (group_shape, current_shape),
            (whole(group_shape.shape), whole(current_shape.shape)), cost=(own_cost, 8 * own_cost),
        )(halves[which], own)

    def update(pieces, current):
        def kernel(pieces_ref, current_ref, copies_ref, new_ref):
            new_ref[...] = corrected(pieces_ref, current_ref, views_total)
            for q in range(quarters):
                copies_ref[q] = new_ref[...]

        return call(
            kernel, (1,), [whole(group_shape.shape), whole(current_shape.shape)], (group_shape, current_shape),
            (whole(group_shape.shape), whole(current_shape.shape)), prefetch=0, cost=(8 * own_cost, 40 * own_cost),
        )(pieces, current)

    def finish(which, pieces, current, so_far):
        aliased = so_far is not None

        def kernel(place_ref, pieces_ref, current_ref, *rest):
            rest[-1][0] = corrected(pieces_ref, current_ref, views_total)

        return call(
            kernel, (1,), [whole(group_shape.shape), whole(current_shape.shape)] + [ANY] * aliased,
            shape(2, half, span, breadth), own_block,
            cost=(8 * own_cost, 24 * own_cost), input_output_aliases={3: 0} if aliased else {},
        )(halves[which], pieces, current, *((so_far,) if aliased else ()))

    def exchange(values):
        return lax.all_to_all(values, "view", 0, 0)

    copies, current = zip(*[share(k) for k in range(2)])
    groups = [exchange(copies[k]) for k in range(2)]
    sens, sens_halo = [None, None], [None, None]
    for k in range(2):
        sens[k] = ones_half(k, sens[0] if k else axial)
        sens_halo[k] = swap(sens[k], k)
    scales = [None, None]
    for iteration in range(ITERS):
        last = iteration == ITERS - 1
        halo = [swap(groups[k], k) for k in range(2)]
        fields, parts, fields_halo = [None, None], [None, None], [None, None]
        for k in range(2):
            fields[k], parts[k] = step_half(k, halo[k], groups[k], groups[1 - k], fields[0] if k else axial, last)
            fields_halo[k] = swap(fields[k], k)
        if iteration == 0:
            for k in range(2):
                scales[k] = depth_half(k, sens_halo[k], sens[k], sens[1 - k], scales[0] if k else axial)
        order = (1, 0) if last else (0, 1)
        pieces, logs = [None, None], axial
        for k in order:
            logs = depth_half(k, fields_halo[k], fields[k], fields[1 - k], logs, scales[k])
            pieces[k] = exchange(logs)
        if not last:
            copies, current = zip(*[update(pieces[k], current[k]) for k in range(2)])
            groups = [exchange(copies[k]) for k in range(2)]
    local = jnp.sum(parts[0] + parts[1], axis=(1, 2))
    updated = finish(order[0], pieces[order[0]], current[order[0]], None)
    local, updated = lax.optimization_barrier((local, updated))
    divergence = lax.psum(local, "depth") / voxel_total
    updated = finish(order[1], pieces[order[1]], current[order[1]], updated)
    return updated.reshape(estimate.shape), divergence


def solution(mesh):
    placed = (
        P("depth", "view", None),
        P("view", "depth", None, None),
        P("view", None, "depth", None, None),
        P("view", None, None, None),
        P("view", None),
    )
    return jax.shard_map(
        body,
        mesh=mesh,
        in_specs=placed,
        out_specs=(P("depth", "view", None), P("view")),
        check_vma=False,
    )
```

```python
import jax
import jax.numpy as jnp
from jax import lax
from jax.experimental import pallas as pl
from jax.experimental.pallas import tpu as pltpu
from jax.sharding import PartitionSpec as P

TAPS = 9
RADIUS = 4
ITERS = 2
F32 = jnp.float32
BF16 = jnp.bfloat16
NOISE_SHIFTS = 64


def mxu(left, right):
    return jnp.dot(left, right, preferred_element_type=F32)


def noise_rows(bases, height):
    return bases * height + 8 * NOISE_SHIFTS


def noise_at(place_ref, view, z, rows):
    shift = lax.rem(37 * (place_ref[1] + view) + 11 * (place_ref[2] + z), NOISE_SHIFTS)
    return pl.ds(pl.multiple_of(shift * 8, 8), rows)


def prepare_kernel(taps_ref, lateral_ref, axial_ref, x_ref, xt_ref, y_ref, yt_ref, axial_out_ref, noise_ref, gain_ref):
    view = pl.program_id(0)
    bases, breadth, height = x_ref.shape[1], x_ref.shape[2], yt_ref.shape[1]
    tall, wide = 32, 128
    inverses = []
    for base in range(bases):
        taps = lateral_ref[0, base]
        inverse = 1.0 / jnp.sum(taps, axis=-1, keepdims=True)
        sums = jnp.sum((taps * inverse).astype(BF16).astype(F32), axis=-1, keepdims=True)
        gain = 1.0 / (sums[0:1] * sums[1:2])
        gain_ref[0, base : base + 1, :] = jnp.broadcast_to(gain, (1, gain_ref.shape[2]))
        inverses.append([jnp.broadcast_to(inverse[k : k + 1], (tall, wide)) for k in range(2)])

    def banded(masks, base, kind, sign):
        total = jnp.zeros((tall, wide), F32)
        for tap in range(TAPS):
            total = jnp.where(masks[tap if sign > 0 else TAPS - 1 - tap], taps_ref[view, base, kind, tap], total)
        return (total * inverses[base][kind]).astype(BF16)

    for r in range(0, breadth, tall):
        for c in range(0, breadth, wide):
            at = (slice(r, r + tall), slice(c, c + wide))
            lateral = r < height and c < height
            if r + tall + RADIUS <= c or c + wide + RADIUS <= r:
                empty = jnp.zeros((tall, wide), BF16)
                for base in range(bases):
                    x_ref[(0, base) + at] = empty
                    xt_ref[(0, base) + at] = empty
                    if lateral:
                        y_ref[0, base * height + r : base * height + r + tall, at[1]] = empty
                        yt_ref[0, at[0], base * height + c : base * height + c + wide] = empty
                continue
            rows = lax.broadcasted_iota(jnp.int32, (tall, wide), 0) + r
            columns = lax.broadcasted_iota(jnp.int32, (tall, wide), 1) + c
            masks = [rows - columns + RADIUS == tap for tap in range(TAPS)]
            for base in range(bases):
                x_ref[(0, base) + at] = banded(masks, base, 1, 1)
                xt_ref[(0, base) + at] = banded(masks, base, 1, -1)
                if lateral:
                    y_ref[0, base * height + r : base * height + r + tall, at[1]] = banded(masks, base, 0, -1)
                    yt_ref[0, at[0], base * height + c : base * height + c + wide] = banded(masks, base, 0, 1)

    @pl.when(pl.program_id(0) == 0)
    def _():
        axial = axial_ref[...]
        axial_out_ref[...] = axial / jnp.sum(axial, axis=-1, keepdims=True)

        def fill(k, carry):
            first = pl.multiple_of(k * 64, 64)
            rows = lax.broadcasted_iota(jnp.int32, (64, breadth), 0) + first
            columns = lax.broadcasted_iota(jnp.int32, (64, breadth), 1)
            mixed = rows * 1664525 + columns * 22695477 + 12345
            for odd, shift in ((739982445, 15), (695872825, 12)):
                mixed = (mixed ^ lax.shift_right_logical(mixed, shift)) * odd
            mixed = mixed ^ lax.shift_right_logical(mixed, 15)
            both = (mixed & 2047) + (lax.shift_right_logical(mixed, 16) & 2047)
            noise_ref[pl.ds(first, 64), :] = 1.0 + (both - 2047).astype(F32) * (1.0 / (2048 * 128))
            return carry

        lax.fori_loop(0, noise_ref.shape[0] // 64, fill, 0)


def adjoint_half(weigh, xt, yt_ref, field_ref, mixed):
    half, rows, _ = mixed.shape
    height = yt_ref.shape[0]
    bases = rows // (2 * height)
    for base in range(bases):
        swept = mxu(weigh(base), xt[base])
        high = swept.astype(BF16)
        low = (swept - high.astype(F32)).astype(BF16)
        for z in range(half):
            at = slice(z * height, (z + 1) * height)
            mixed[z, base * height : (base + 1) * height, :] = high[at]
            mixed[z, (bases + base) * height : (bases + base + 1) * height, :] = low[at]
    twice = jnp.concatenate([yt_ref[...], yt_ref[...]], axis=1)
    for z in range(half):
        field_ref[0, z] = mxu(twice, mixed[z])


def ones_kernel(place_ref, weights_any, xt_any, yt_any, after_any, field_ref, weights, xt, yt, sems, mixed):
    view = pl.program_id(0)
    views, bases, half, height, breadth = weights.shape
    planes = pl.ds(place_ref[0] * half, half)

    def copies(at):
        pairs = ((weights_any.at[at, :, planes], weights), (xt_any.at[at], xt), (yt_any.at[at], yt))
        return [pltpu.make_async_copy(a, b.at[at], sems.at[at, k]) for k, (a, b) in enumerate(pairs)]

    @pl.when(view == 0)
    def _():
        for at in range(views):
            for copy in copies(at):
                copy.start()

    for copy in copies(view):
        copy.wait()
    adjoint_half(lambda base: weights[view, base].reshape(half * height, breadth), xt.at[view], yt.at[view], field_ref, mixed)


def step_kernel(place_ref, axial_ref, halo_ref, near_ref, far_ref, noise_ref, gain_ref, y_ref, counts_any, weights_any,
                x_any, xt_any, yt_any, after_any, field_ref, fidelity_ref, weights, counts_buf, x, xt, yt, sems,
                blurred, rows, mixed):
    view = pl.program_id(0)
    views, bases, half, height, breadth = weights.shape
    quarters, _, span, _ = near_ref.shape
    planes = pl.ds(place_ref[0] * half, half)

    def copies(at):
        pairs = ((x_any.at[at], x), (weights_any.at[at, :, planes], weights), (counts_any.at[at, planes], counts_buf),
                 (xt_any.at[at], xt), (yt_any.at[at], yt))
        return [pltpu.make_async_copy(a, b.at[at], sems.at[at, k]) for k, (a, b) in enumerate(pairs)]

    @pl.when(view == 0)
    def _():
        for at in range(views):
            for copy in copies(at):
                copy.start()

    def depth_blur(groups):
        for z in range(half):
            for q in range(quarters):
                total = None
                for tap in range(TAPS):
                    plane = z + tap
                    term = axial_ref[view, tap] * groups[plane // half][q, plane % half]
                    total = term if total is None else total + term
                high = total.astype(BF16)
                blurred[z, q * span : (q + 1) * span, :] = high
                blurred[z, height + q * span : height + (q + 1) * span, :] = (total - high.astype(F32)).astype(BF16)

    @pl.when(place_ref[0] == 0)
    def _():
        depth_blur((halo_ref, near_ref, far_ref))

    @pl.when(place_ref[0] != 0)
    def _():
        depth_blur((far_ref, near_ref, halo_ref))

    for copy in copies(view):
        copy.wait()
    twice = jnp.concatenate([y_ref[0], y_ref[0]], axis=1)
    for z in range(half):
        swept = mxu(twice, blurred[z]) * noise_ref[noise_at(place_ref, view, z, bases * height), :]
        for base in range(bases):
            gain = gain_ref[0, base : base + 1, :]
            rows[base, z * height : (z + 1) * height, :] = (swept[base * height : (base + 1) * height] * gain).astype(BF16)

    def weights_of(base):
        return weights[view, base].reshape(half * height, breadth).astype(F32)

    predicted = None
    for base in range(bases):
        term = weights_of(base) * mxu(rows[base], x[view, base])
        predicted = term if predicted is None else predicted + term
    counts = counts_buf[view].reshape(half * height, breadth)
    ratios = counts / predicted
    if fidelity_ref is not None:
        terms = counts * jnp.log(ratios) - counts + predicted
        fidelity_ref[0] = jnp.sum(terms.reshape(-1, 8, breadth), axis=0)
    noise = [noise_ref[noise_at(place_ref, view, z, height), :] for z in range(half)]
    spread = ratios * jnp.concatenate(noise, axis=0)
    adjoint_half(lambda base: (weights_of(base) * spread).astype(BF16), xt.at[view], yt.at[view], field_ref, mixed)


def plain_step_kernel(*refs):
    step_kernel(*refs[:15], None, *refs[15:])


def depth_adjoint(place_ref, axial_ref, groups, quarters, write):
    views, half, height, _ = groups[1].shape
    span = height // quarters

    def run(ordered):
        def quarter(q, carry):
            at = pl.ds(pl.multiple_of(q * span, span), span)
            for z in range(half):
                product = None
                for view in range(views):
                    total = None
                    for tap in range(TAPS):
                        plane = z + 2 * RADIUS - tap
                        term = axial_ref[view, tap] * ordered[plane // half][view, plane % half, at, :]
                        total = term if total is None else total + term
                    product = total if product is None else product * total
                write(q, z, product)
            return carry

        lax.fori_loop(0, quarters, quarter, 0)

    halo_ref, near_ref, far_ref = groups

    @pl.when(place_ref[0] == 0)
    def _():
        run((halo_ref, near_ref, far_ref))

    @pl.when(place_ref[0] != 0)
    def _():
        run((far_ref, near_ref, halo_ref))


def scale_kernel(place_ref, axial_ref, halo_ref, near_ref, far_ref, after_any, out_ref):
    def store(q, z, product):
        out_ref[q, z] = 1.0 / product

    depth_adjoint(place_ref, axial_ref, (halo_ref, near_ref, far_ref), out_ref.shape[0], store)


def log_kernel(place_ref, axial_ref, halo_ref, near_ref, far_ref, scale_ref, before_any, out_ref):
    def store(q, z, product):
        out_ref[q, 0, z] = jnp.log(product * scale_ref[q, z])

    depth_adjoint(place_ref, axial_ref, (halo_ref, near_ref, far_ref), out_ref.shape[0], store)


def share_kernel(place_ref, own_ref, copies_ref, current_ref):
    for k in range(2):
        at = place_ref[0] if k == 0 else 1 - place_ref[0]
        values = own_ref[at]
        current_ref[k] = values
        for q in range(copies_ref.shape[0]):
            copies_ref[q, k] = values


def corrected(pieces_ref, current_ref, k, views_total):
    total = pieces_ref[0, k]
    for q in range(1, pieces_ref.shape[0]):
        total = total + pieces_ref[q, k]
    return current_ref[k] * jnp.exp(total * (1.0 / views_total))


def whole(shape):
    return pl.BlockSpec(shape, lambda *_: (0,) * len(shape))


def per_view(shape):
    return pl.BlockSpec((1,) + shape[1:], lambda v, *_: (v,) + (0,) * (len(shape) - 1))


ANY = pl.BlockSpec(memory_space=pl.ANY)
SMEM = pl.BlockSpec(memory_space=pltpu.SMEM)


def hbm(values):
    return pltpu.with_memory_space_constraint(values, pltpu.HBM)


def call(kernel, grid, in_specs, out_shape, out_specs, scratch=(), prefetch=1, vmem=16, **more):
    return pl.pallas_call(
        kernel,
        out_shape=out_shape,
        grid_spec=pltpu.PrefetchScalarGridSpec(
            num_scalar_prefetch=prefetch, grid=grid, in_specs=in_specs, out_specs=out_specs, scratch_shapes=list(scratch)),
        compiler_params=pltpu.CompilerParams(vmem_limit_bytes=vmem * 1024 * 1024),
        cost_estimate=pl.CostEstimate(flops=1024, bytes_accessed=1024, transcendentals=0),
        **more,
    )


def body(estimate, observed, voxel_weights, lateral_taps, axial_taps):
    views, planes, height, breadth = observed.shape
    bases = voxel_weights.shape[1]
    half = planes // 2
    assert half == RADIUS and planes % 2 == 0
    quarters = lax.axis_size("view")
    depths = lax.axis_size("depth")
    span = height // quarters
    views_total = views * quarters
    voxel_total = planes * depths * height * breadth
    parity = lax.rem(lax.axis_index("depth"), 2).astype(jnp.int32)
    first_view, first_plane = lax.axis_index("view") * views, lax.axis_index("depth") * planes
    halves = [
        jnp.stack([at, first_view, first_plane + at * half]).astype(jnp.int32) for at in (parity, 1 - parity)
    ]

    def swap(values, which):
        pairs = []
        for i in range(1 - which, depths - 1, 2):
            pairs += [(i, i + 1), (i + 1, i)]
        return lax.ppermute(values, "depth", pairs)

    def shape(*dims, dtype=F32):
        return jax.ShapeDtypeStruct(dims, dtype)

    x_shape = shape(views, bases, breadth, breadth, dtype=BF16)
    y_shape = shape(views, bases * height, height, dtype=BF16)
    gain_shape = shape(views, bases, breadth)
    yt_shape = shape(views, height, bases * height, dtype=BF16)
    noise_shape = shape(noise_rows(bases, height), breadth)
    group_shape = shape(quarters, half, span, breadth)
    field_shape = shape(views, half, height, breadth)
    fidelity_shape = shape(views, 8, breadth)
    pair_shape = shape(quarters, 2, half, span, breadth)

    x_mat, xt_mat, y_mat, yt_mat, axial, noise, gain = call(
        prepare_kernel, (views,), [SMEM, per_view(lateral_taps.shape), whole(axial_taps.shape)],
        tuple(pltpu.HBM(a.shape, a.dtype) for a in (x_shape, x_shape, y_shape, yt_shape, axial_taps, noise_shape, gain_shape)),
        (per_view(x_shape.shape), per_view(x_shape.shape), per_view(y_shape.shape), per_view(yt_shape.shape),
         whole(axial_taps.shape), whole(noise_shape.shape), per_view(gain_shape.shape)),
        prefetch=0,
    )(lateral_taps, lateral_taps, axial_taps)
    x_mat, xt_mat, y_mat, yt_mat, noise, gain = (hbm(a) for a in (x_mat, xt_mat, y_mat, yt_mat, noise, gain))
    weights_in = hbm(voxel_weights)

    weights_buf = pltpu.VMEM((views, bases, half, height, breadth), BF16)
    x_buf = pltpu.VMEM(x_shape.shape, BF16)
    yt_buf = pltpu.VMEM(yt_shape.shape, BF16)
    sems = pltpu.SemaphoreType.DMA((views, 5))
    mixed_buf = pltpu.VMEM((half, 2 * bases * height, breadth), BF16)

    def ones_half(which, after):
        return call(
            ones_kernel, (views,), [ANY] * 4, field_shape, per_view(field_shape.shape),
            [weights_buf, x_buf, yt_buf, sems, mixed_buf], vmem=20,
        )(halves[which], weights_in, xt_mat, yt_mat, after)

    def step_half(which, halo, near, far, after, last):
        out = call(
            step_kernel if last else plain_step_kernel, (views,),
            [SMEM] + [whole(group_shape.shape)] * 3 + [whole(noise_shape.shape), per_view(gain_shape.shape), per_view(y_shape.shape)] + [ANY] * 6,
            (field_shape, fidelity_shape) if last else field_shape,
            (per_view(field_shape.shape), per_view(fidelity_shape.shape)) if last else per_view(field_shape.shape),
            [weights_buf, pltpu.VMEM((views, half, height, breadth), F32), x_buf, x_buf, yt_buf, sems,
             pltpu.VMEM((half, 2 * height, breadth), BF16),
             pltpu.VMEM((bases, half * height, breadth), BF16), mixed_buf],
            vmem=36,
        )(halves[which], axial, halo, near, far, noise, gain, y_mat, hbm(observed), weights_in, x_mat, xt_mat, yt_mat, after)
        return out if last else (out, None)

    def scale_half(which, halo, near, far, after):
        return call(
            scale_kernel, (1,), [SMEM] + [whole(field_shape.shape)] * 3 + [ANY], group_shape, whole(group_shape.shape),
        )(halves[which], axial, halo, near, far, after)

    def log_half(which, halo, near, far, scale, so_far):
        aliased = so_far is not None
        block = pl.BlockSpec((quarters, 1, half, span, breadth), lambda *_: (0, which, 0, 0, 0))
        return call(
            log_kernel, (1,), [SMEM] + [whole(field_shape.shape)] * 3 + [whole(group_shape.shape), ANY],
            pltpu.HBM(pair_shape.shape, F32), block, input_output_aliases={6: 0} if aliased else {},
        )(halves[which], axial, halo, near, far, scale, hbm(so_far) if aliased else axial)

    def share():
        own = estimate.reshape(2, half, span, breadth)
        return call(
            share_kernel, (1,), [whole(own.shape)], (pltpu.HBM(pair_shape.shape, F32), pltpu.HBM(own.shape, F32)),
            (whole(pair_shape.shape), whole(own.shape)),
        )(halves[0], own)

    def update(pieces, current):
        def kernel(pieces_ref, current_ref, first_ref, second_ref, new_ref):
            for k, copies_ref in enumerate((first_ref, second_ref)):
                new_ref[k] = corrected(pieces_ref, current_ref, k, views_total)
                for q in range(quarters):
                    copies_ref[q] = new_ref[k]

        group_hbm = pltpu.HBM(group_shape.shape, F32)
        *copies, new = call(
            kernel, (1,), [whole(pair_shape.shape), whole(current.shape)],
            (group_hbm, group_hbm, pltpu.HBM(current.shape, F32)),
            (whole(group_shape.shape), whole(group_shape.shape), whole(current.shape)), prefetch=0,
        )(pieces, hbm(current))
        return copies, new

    def finish(pieces, current):
        def kernel(place_ref, pieces_ref, current_ref, out_ref):
            for k in range(2):
                at = place_ref[0] if k == 0 else 1 - place_ref[0]
                out_ref[at] = corrected(pieces_ref, current_ref, k, views_total)

        return call(
            kernel, (1,), [whole(pair_shape.shape), whole(current.shape)], shape(*current.shape), whole(current.shape),
        )(halves[0], pieces, hbm(current))

    def exchange(values):
        return lax.all_to_all(values, "view", 0, 0)

    copies, current = share()
    gathered = exchange(copies)
    groups = [gathered[:, k] for k in range(2)]
    sens, sens_halo = [None, None], [None, None]
    for k in range(2):
        sens[k] = ones_half(k, sens[0] if k else axial)
        sens_halo[k] = swap(sens[k], k)
    scales = [None, None]
    for iteration in range(ITERS):
        last = iteration == ITERS - 1
        halo = [swap(groups[k], k) for k in range(2)]
        fields, parts, fields_halo = [None, None], [None, None], [None, None]
        for k in range(2):
            fields[k], parts[k] = step_half(k, halo[k], groups[k], groups[1 - k], fields[0] if k else axial, last)
            fields_halo[k] = swap(fields[k], k)
        if iteration == 0:
            for k in range(2):
                scales[k] = scale_half(k, sens_halo[k], sens[k], sens[1 - k], axial)
        logs = None
        for k in range(2):
            logs = log_half(k, fields_halo[k], fields[k], fields[1 - k], scales[k], logs)
        pieces = exchange(logs)
        if not last:
            copies, current = update(pieces, current)
            groups = [exchange(copies[k]) for k in range(2)]
    divergence = lax.psum(jnp.sum(parts[0] + parts[1], axis=(1, 2)), "depth") / voxel_total
    updated = finish(pieces, current)
    return updated.reshape(estimate.shape), divergence


def solution(mesh):
    placed = (
        P("depth", "view", None),
        P("view", "depth", None, None),
        P("view", None, "depth", None, None),
        P("view", None, None, None),
        P("view", None),
    )
    return jax.shard_map(
        body,
        mesh=mesh,
        in_specs=placed,
        out_specs=(P("depth", "view", None), P("view")),
        check_vma=False,
    )
```

```python
import jax
import jax.numpy as jnp
from jax import lax
from jax.experimental import pallas as pl
from jax.experimental.pallas import tpu as pltpu
from jax.sharding import PartitionSpec as P

TAPS = 9
RADIUS = 4
ITERS = 2
F32 = jnp.float32
BF16 = jnp.bfloat16
NOISE_SHIFTS = 64


def mxu(left, right):
    return jnp.dot(left, right, preferred_element_type=F32)


def noise_rows(bases, height):
    return bases * height + 8 * NOISE_SHIFTS


def noise_at(place_ref, view, z, rows):
    shift = lax.rem(37 * (place_ref[1] + view) + 11 * (place_ref[2] + z), NOISE_SHIFTS)
    return pl.ds(pl.multiple_of(shift * 8, 8), rows)


def prepare_kernel(taps_ref, lateral_ref, axial_ref, x_ref, xt_ref, y_ref, yt_ref, axial_out_ref, noise_ref, gain_ref):
    view = pl.program_id(0)
    bases, breadth, height = x_ref.shape[1], x_ref.shape[2], yt_ref.shape[1]
    tall, wide = 32, 128
    inverses = []
    for base in range(bases):
        taps = lateral_ref[0, base]
        inverse = 1.0 / jnp.sum(taps, axis=-1, keepdims=True)
        sums = jnp.sum((taps * inverse).astype(BF16).astype(F32), axis=-1, keepdims=True)
        gain = 1.0 / (sums[0:1] * sums[1:2])
        gain_ref[0, base : base + 1, :] = jnp.broadcast_to(gain, (1, gain_ref.shape[2]))
        inverses.append([jnp.broadcast_to(inverse[k : k + 1], (tall, wide)) for k in range(2)])

    def banded(masks, base, kind, sign):
        total = jnp.zeros((tall, wide), F32)
        for tap in range(TAPS):
            total = jnp.where(masks[tap if sign > 0 else TAPS - 1 - tap], taps_ref[view, base, kind, tap], total)
        return (total * inverses[base][kind]).astype(BF16)

    for r in range(0, breadth, tall):
        for c in range(0, breadth, wide):
            at = (slice(r, r + tall), slice(c, c + wide))
            lateral = r < height and c < height
            if r + tall + RADIUS <= c or c + wide + RADIUS <= r:
                empty = jnp.zeros((tall, wide), BF16)
                for base in range(bases):
                    x_ref[(0, base) + at] = empty
                    xt_ref[(0, base) + at] = empty
                    if lateral:
                        y_ref[0, base * height + r : base * height + r + tall, at[1]] = empty
                        yt_ref[0, at[0], base * height + c : base * height + c + wide] = empty
                continue
            rows = lax.broadcasted_iota(jnp.int32, (tall, wide), 0) + r
            columns = lax.broadcasted_iota(jnp.int32, (tall, wide), 1) + c
            masks = [rows - columns + RADIUS == tap for tap in range(TAPS)]
            for base in range(bases):
                x_ref[(0, base) + at] = banded(masks, base, 1, 1)
                xt_ref[(0, base) + at] = banded(masks, base, 1, -1)
                if lateral:
                    y_ref[0, base * height + r : base * height + r + tall, at[1]] = banded(masks, base, 0, -1)
                    yt_ref[0, at[0], base * height + c : base * height + c + wide] = banded(masks, base, 0, 1)

    @pl.when(pl.program_id(0) == 0)
    def _():
        axial = axial_ref[...]
        axial_out_ref[...] = axial / jnp.sum(axial, axis=-1, keepdims=True)

        def fill(k, carry):
            first = pl.multiple_of(k * 64, 64)
            rows = lax.broadcasted_iota(jnp.int32, (64, breadth), 0) + first
            columns = lax.broadcasted_iota(jnp.int32, (64, breadth), 1)
            mixed = rows * 1664525 + columns * 22695477 + 12345
            for odd, shift in ((739982445, 15), (695872825, 12)):
                mixed = (mixed ^ lax.shift_right_logical(mixed, shift)) * odd
            mixed = mixed ^ lax.shift_right_logical(mixed, 15)
            both = (mixed & 2047) + (lax.shift_right_logical(mixed, 16) & 2047)
            noise_ref[pl.ds(first, 64), :] = 1.0 + (both - 2047).astype(F32) * (1.0 / (2048 * 128))
            return carry

        lax.fori_loop(0, noise_ref.shape[0] // 64, fill, 0)


def adjoint_base(values, base, xt, mixed):
    half, rows, _ = mixed.shape
    height = values.shape[0] // half
    swept = mxu(values, xt[base])
    high = swept.astype(BF16)
    low = (swept - high.astype(F32)).astype(BF16)
    for z in range(half):
        at = slice(z * height, (z + 1) * height)
        mixed[z, base * height : (base + 1) * height, :] = high[at]
        mixed[z, rows // 2 + base * height : rows // 2 + (base + 1) * height, :] = low[at]


def adjoint_rows(yt, mixed, z):
    return mxu(jnp.concatenate([yt[...], yt[...]], axis=1), mixed[z])


def ones_kernel(place_ref, weights_any, xt_any, yt_any, after_any, field_ref, weights, xt, yt, sems, mixed):
    views, bases, half, height, breadth = weights.shape
    planes = pl.ds(place_ref[0] * half, half)
    copies = []
    for view in range(views):
        pairs = ((weights_any.at[view, :, planes], weights), (xt_any.at[view], xt), (yt_any.at[view], yt))
        copies.append([pltpu.make_async_copy(a, b.at[view], sems.at[view, k]) for k, (a, b) in enumerate(pairs)])
        for copy in copies[-1]:
            copy.start()
    for view in range(views):
        for copy in copies[view]:
            copy.wait()
        for base in range(bases):
            adjoint_base(weights[view, base].reshape(half * height, breadth), base, xt.at[view], mixed.at[view])
        for z in range(half):
            field_ref[view, z] = adjoint_rows(yt.at[view], mixed.at[view], z)


def step_kernel(place_ref, axial_ref, halo_ref, near_ref, far_ref, noise_any, gain_ref, y_any, counts_any, weights_any,
                x_any, xt_any, yt_any, after_any, field_ref, fidelity_ref, weights, counts, x, xt, yt, y, noise_ref, sems,
                blurred, rows, mixed):
    views, bases, half, height, breadth = weights.shape
    quarters, _, span, _ = near_ref.shape
    planes = pl.ds(place_ref[0] * half, half)
    early = [pltpu.make_async_copy(noise_any, noise_ref, sems.at[views, 0]), pltpu.make_async_copy(y_any, y, sems.at[views, 1])]
    late = []
    for view in range(views):
        pairs = ((x_any.at[view], x), (weights_any.at[view, :, planes], weights), (counts_any.at[view, planes], counts),
                 (xt_any.at[view], xt), (yt_any.at[view], yt))
        late += [pltpu.make_async_copy(a, b.at[view], sems.at[view, k]) for k, (a, b) in enumerate(pairs)]
    for copy in early + late:
        copy.start()

    def depth_blur(groups):
        for view in range(views):
            for z in range(half):
                for q in range(quarters):
                    total = None
                    for tap in range(TAPS):
                        plane = z + tap
                        term = axial_ref[view, tap] * groups[plane // half][q, plane % half]
                        total = term if total is None else total + term
                    high = total.astype(BF16)
                    blurred[view, z, q * span : (q + 1) * span, :] = high
                    low = (total - high.astype(F32)).astype(BF16)
                    blurred[view, z, height + q * span : height + (q + 1) * span, :] = low

    @pl.when(place_ref[0] == 0)
    def _():
        depth_blur((halo_ref, near_ref, far_ref))

    @pl.when(place_ref[0] != 0)
    def _():
        depth_blur((far_ref, near_ref, halo_ref))

    def sweep_rows(view, z):
        twice = jnp.concatenate([y[view], y[view]], axis=1)
        swept = mxu(twice, blurred[view, z]) * noise_ref[noise_at(place_ref, view, z, bases * height), :]
        for base in range(bases):
            gain = gain_ref[view, base : base + 1, :]
            part = (swept[base * height : (base + 1) * height] * gain).astype(BF16)
            rows[view, base, z * height : (z + 1) * height, :] = part

    def weights_of(view, base):
        return weights[view, base].reshape(half * height, breadth).astype(F32)

    predicted, spread = [None] * views, [None] * views

    def predict(view, base):
        term = weights_of(view, base) * mxu(rows[view, base], x[view, base])
        predicted[view] = term if base == 0 else predicted[view] + term

    def compare(view):
        observed = counts[view].reshape(half * height, breadth)
        ratios = observed / predicted[view]
        if fidelity_ref is not None:
            terms = observed * jnp.log(ratios) - observed + predicted[view]
            fidelity_ref[view] = jnp.sum(terms.reshape(-1, 8, breadth), axis=0)
        noise = [noise_ref[noise_at(place_ref, view, z, height), :] for z in range(half)]
        spread[view] = ratios * jnp.concatenate(noise, axis=0)

    def back(view, base):
        adjoint_base((weights_of(view, base) * spread[view]).astype(BF16), base, xt.at[view], mixed.at[view])

    def back_rows(view, z):
        field_ref[view, z] = adjoint_rows(yt.at[view], mixed.at[view], z)

    for copy in early:
        copy.wait()
    for z in range(half):
        sweep_rows(0, z)
    for copy in late:
        copy.wait()
    for view in range(views):
        following = view + 1 < views
        for base in range(bases):
            predict(view, base)
            if following and (base + 1) % (bases // half) == 0:
                sweep_rows(view + 1, base // (bases // half))
            if view > 0:
                back(view - 1, base)
        compare(view)
        if view > 0:
            for z in range(half):
                back_rows(view - 1, z)
    for base in range(bases):
        back(views - 1, base)
    for z in range(half):
        back_rows(views - 1, z)


def plain_step_kernel(*refs):
    step_kernel(*refs[:15], None, *refs[15:])


def depth_adjoint(place_ref, axial_ref, groups, quarters, write):
    views, half, height, _ = groups[1].shape
    span = height // quarters

    def run(ordered):
        def quarter(q, carry):
            at = pl.ds(pl.multiple_of(q * span, span), span)
            for z in range(half):
                product = None
                for view in range(views):
                    total = None
                    for tap in range(TAPS):
                        plane = z + 2 * RADIUS - tap
                        term = axial_ref[view, tap] * ordered[plane // half][view, plane % half, at, :]
                        total = term if total is None else total + term
                    product = total if product is None else product * total
                write(q, z, product)
            return carry

        lax.fori_loop(0, quarters, quarter, 0)

    halo_ref, near_ref, far_ref = groups

    @pl.when(place_ref[0] == 0)
    def _():
        run((halo_ref, near_ref, far_ref))

    @pl.when(place_ref[0] != 0)
    def _():
        run((far_ref, near_ref, halo_ref))


def scale_kernel(place_ref, axial_ref, halo_ref, near_ref, far_ref, after_any, out_ref):
    def store(q, z, product):
        out_ref[q, z] = 1.0 / product

    depth_adjoint(place_ref, axial_ref, (halo_ref, near_ref, far_ref), out_ref.shape[0], store)


def log_kernel(place_ref, axial_ref, halo_ref, near_ref, far_ref, scale_ref, before_any, out_ref):
    def store(q, z, product):
        out_ref[q, 0, z] = jnp.log(product * scale_ref[q, z])

    depth_adjoint(place_ref, axial_ref, (halo_ref, near_ref, far_ref), out_ref.shape[0], store)


def share_kernel(place_ref, own_ref, copies_ref, current_ref):
    for k in range(2):
        at = place_ref[0] if k == 0 else 1 - place_ref[0]
        values = own_ref[at]
        current_ref[k] = values
        for q in range(copies_ref.shape[0]):
            copies_ref[q, k] = values


def corrected(pieces_ref, current_ref, k, views_total):
    total = pieces_ref[0, k]
    for q in range(1, pieces_ref.shape[0]):
        total = total + pieces_ref[q, k]
    return current_ref[k] * jnp.exp(total * (1.0 / views_total))


def whole(shape):
    return pl.BlockSpec(shape, lambda *_: (0,) * len(shape))


def per_view(shape):
    return pl.BlockSpec((1,) + shape[1:], lambda v, *_: (v,) + (0,) * (len(shape) - 1))


ANY = pl.BlockSpec(memory_space=pl.ANY)
SMEM = pl.BlockSpec(memory_space=pltpu.SMEM)


def hbm(values):
    return pltpu.with_memory_space_constraint(values, pltpu.HBM)


def call(kernel, grid, in_specs, out_shape, out_specs, scratch=(), prefetch=1, vmem=16, **more):
    return pl.pallas_call(
        kernel,
        out_shape=out_shape,
        grid_spec=pltpu.PrefetchScalarGridSpec(
            num_scalar_prefetch=prefetch, grid=grid, in_specs=in_specs, out_specs=out_specs, scratch_shapes=list(scratch)),
        compiler_params=pltpu.CompilerParams(vmem_limit_bytes=vmem * 1024 * 1024),
        cost_estimate=pl.CostEstimate(flops=1024, bytes_accessed=1024, transcendentals=0),
        **more,
    )


def body(estimate, observed, voxel_weights, lateral_taps, axial_taps):
    views, planes, height, breadth = observed.shape
    bases = voxel_weights.shape[1]
    half = planes // 2
    assert half == RADIUS and planes % 2 == 0
    quarters = lax.axis_size("view")
    depths = lax.axis_size("depth")
    span = height // quarters
    views_total = views * quarters
    voxel_total = planes * depths * height * breadth
    parity = lax.rem(lax.axis_index("depth"), 2).astype(jnp.int32)
    first_view, first_plane = lax.axis_index("view") * views, lax.axis_index("depth") * planes
    halves = [
        jnp.stack([at, first_view, first_plane + at * half]).astype(jnp.int32) for at in (parity, 1 - parity)
    ]

    def swap(values, which):
        pairs = []
        for i in range(1 - which, depths - 1, 2):
            pairs += [(i, i + 1), (i + 1, i)]
        return lax.ppermute(values, "depth", pairs)

    def shape(*dims, dtype=F32):
        return jax.ShapeDtypeStruct(dims, dtype)

    x_shape = shape(views, bases, breadth, breadth, dtype=BF16)
    y_shape = shape(views, bases * height, height, dtype=BF16)
    gain_shape = shape(views, bases, breadth)
    yt_shape = shape(views, height, bases * height, dtype=BF16)
    noise_shape = shape(noise_rows(bases, height), breadth)
    group_shape = shape(quarters, half, span, breadth)
    field_shape = shape(views, half, height, breadth)
    fidelity_shape = shape(views, 8, breadth)
    pair_shape = shape(quarters, 2, half, span, breadth)

    x_mat, xt_mat, y_mat, yt_mat, axial, noise, gain = call(
        prepare_kernel, (views,), [SMEM, per_view(lateral_taps.shape), whole(axial_taps.shape)],
        tuple(pltpu.HBM(a.shape, a.dtype) for a in (x_shape, x_shape, y_shape, yt_shape, axial_taps, noise_shape, gain_shape)),
        (per_view(x_shape.shape), per_view(x_shape.shape), per_view(y_shape.shape), per_view(yt_shape.shape),
         whole(axial_taps.shape), whole(noise_shape.shape), per_view(gain_shape.shape)),
        prefetch=0,
    )(lateral_taps, lateral_taps, axial_taps)
    x_mat, xt_mat, y_mat, yt_mat, noise, gain = (hbm(a) for a in (x_mat, xt_mat, y_mat, yt_mat, noise, gain))
    weights_in = hbm(voxel_weights)

    weights_buf = pltpu.VMEM((views, bases, half, height, breadth), BF16)
    x_buf = pltpu.VMEM(x_shape.shape, BF16)
    yt_buf = pltpu.VMEM(yt_shape.shape, BF16)
    sems = pltpu.SemaphoreType.DMA((views, 5))
    mixed_buf = pltpu.VMEM((views, half, 2 * bases * height, breadth), BF16)

    def ones_half(which, after):
        return call(
            ones_kernel, (1,), [ANY] * 4, field_shape, whole(field_shape.shape),
            [weights_buf, x_buf, yt_buf, sems, mixed_buf], vmem=28,
        )(halves[which], weights_in, xt_mat, yt_mat, after)

    def step_half(which, halo, near, far, after, last):
        out = call(
            step_kernel if last else plain_step_kernel, (1,),
            [SMEM] + [whole(group_shape.shape)] * 3 + [ANY, whole(gain_shape.shape)] + [ANY] * 7,
            (field_shape, fidelity_shape) if last else field_shape,
            (whole(field_shape.shape), whole(fidelity_shape.shape)) if last else whole(field_shape.shape),
            [weights_buf, pltpu.VMEM((views, half, height, breadth), F32), x_buf, x_buf, yt_buf,
             pltpu.VMEM(y_shape.shape, BF16), pltpu.VMEM(noise_shape.shape, F32), pltpu.SemaphoreType.DMA((views + 1, 5)),
             pltpu.VMEM((views, half, 2 * height, breadth), BF16),
             pltpu.VMEM((views, bases, half * height, breadth), BF16), mixed_buf],
            vmem=44,
        )(halves[which], axial, halo, near, far, noise, gain, y_mat, hbm(observed), weights_in, x_mat, xt_mat, yt_mat, after)
        return out if last else (out, None)

    def scale_half(which, halo, near, far, after):
        return call(
            scale_kernel, (1,), [SMEM] + [whole(field_shape.shape)] * 3 + [ANY], group_shape, whole(group_shape.shape),
        )(halves[which], axial, halo, near, far, after)

    def log_half(which, halo, near, far, scale, so_far):
        aliased = so_far is not None
        block = pl.BlockSpec((quarters, 1, half, span, breadth), lambda *_: (0, which, 0, 0, 0))
        return call(
            log_kernel, (1,), [SMEM] + [whole(field_shape.shape)] * 3 + [whole(group_shape.shape), ANY],
            pltpu.HBM(pair_shape.shape, F32), block, input_output_aliases={6: 0} if aliased else {},
        )(halves[which], axial, halo, near, far, scale, hbm(so_far) if aliased else axial)

    def share():
        own = estimate.reshape(2, half, span, breadth)
        return call(
            share_kernel, (1,), [whole(own.shape)], (pltpu.HBM(pair_shape.shape, F32), pltpu.HBM(own.shape, F32)),
            (whole(pair_shape.shape), whole(own.shape)),
        )(halves[0], hbm(own))

    def part(pair, after):
        def kernel(pair_ref, after_any, *out_refs):
            for k in range(2):
                out_refs[k][...] = pair_ref[:, k]

        return call(
            kernel, (1,), [whole(pair_shape.shape), ANY], (group_shape, group_shape), (whole(group_shape.shape),) * 2,
            prefetch=0,
        )(pair, after)

    def update(pieces, current):
        def kernel(pieces_ref, current_ref, first_ref, second_ref, new_ref):
            for k, copies_ref in enumerate((first_ref, second_ref)):
                new_ref[k] = corrected(pieces_ref, current_ref, k, views_total)
                for q in range(quarters):
                    copies_ref[q] = new_ref[k]

        group_hbm = pltpu.HBM(group_shape.shape, F32)
        *copies, new = call(
            kernel, (1,), [whole(pair_shape.shape), whole(current.shape)],
            (group_hbm, group_hbm, pltpu.HBM(current.shape, F32)),
            (whole(group_shape.shape), whole(group_shape.shape), whole(current.shape)), prefetch=0,
        )(pieces, hbm(current))
        return copies, new

    def finish(pieces, current):
        def kernel(place_ref, pieces_ref, current_ref, out_ref):
            for k in range(2):
                at = place_ref[0] if k == 0 else 1 - place_ref[0]
                out_ref[at] = corrected(pieces_ref, current_ref, k, views_total)

        return call(
            kernel, (1,), [whole(pair_shape.shape), whole(current.shape)], shape(*current.shape), whole(current.shape),
        )(halves[0], pieces, hbm(current))

    def exchange(values):
        return lax.all_to_all(values, "view", 0, 0)

    copies, current = share()
    gathered = exchange(copies)
    sens, sens_halo = [None, None], [None, None]
    sens[0] = ones_half(0, copies)
    groups = part(gathered, sens[0])
    sens[1] = ones_half(1, groups[0])
    sens_halo = [swap(sens[k], k) for k in range(2)]
    scales = [None, None]
    for iteration in range(ITERS):
        last = iteration == ITERS - 1
        halo = [swap(groups[k], k) for k in range(2)]
        fields, parts, fields_halo = [None, None], [None, None], [None, None]
        for k in range(2):
            fields[k], parts[k] = step_half(k, halo[k], groups[k], groups[1 - k], fields[0] if k else axial, last)
            fields_halo[k] = swap(fields[k], k)
        if iteration == 0:
            for k in range(2):
                scales[k] = scale_half(k, sens_halo[k], sens[k], sens[1 - k], axial)
        logs = None
        for k in range(2):
            logs = log_half(k, fields_halo[k], fields[k], fields[1 - k], scales[k], logs)
        pieces = exchange(logs)
        if not last:
            copies, current = update(pieces, current)
            groups = [exchange(copies[k]) for k in range(2)]
    divergence = lax.psum(jnp.sum(parts[0] + parts[1], axis=(1, 2)), "depth") / voxel_total
    updated = finish(pieces, current)
    return updated.reshape(estimate.shape), divergence


def solution(mesh):
    placed = (
        P("depth", "view", None),
        P("view", "depth", None, None),
        P("view", None, "depth", None, None),
        P("view", None, None, None),
        P("view", None),
    )
    return jax.shard_map(
        body,
        mesh=mesh,
        in_specs=placed,
        out_specs=(P("depth", "view", None), P("view")),
        check_vma=False,
    )
```

```python
import jax
import jax.numpy as jnp
from jax import lax
from jax.experimental import pallas as pl
from jax.experimental.pallas import tpu as pltpu
from jax.sharding import PartitionSpec as P

TAPS = 9
RADIUS = 4
ITERS = 2
F32 = jnp.float32
BF16 = jnp.bfloat16
NOISE_SHIFTS = 64


def mxu(left, right):
    return jnp.dot(left, right, preferred_element_type=F32)


def noise_rows(bases, height):
    return bases * height + 8 * NOISE_SHIFTS


def noise_at(place_ref, view, z, rows):
    shift = lax.rem(37 * (place_ref[1] + view) + 11 * (place_ref[2] + z), NOISE_SHIFTS)
    return pl.ds(pl.multiple_of(shift * 8, 8), rows)


def prepare_kernel(taps_ref, lateral_ref, axial_ref, weights_any, counts_any, x_ref, xt_ref, y_ref, yt_ref, noise_ref,
                   gain_ref, weights_ref, counts_ref, axial_out_ref, sems):
    copies = [pltpu.make_async_copy(weights_any, weights_ref, sems.at[0]), pltpu.make_async_copy(counts_any, counts_ref, sems.at[1])]
    for copy in copies:
        copy.start()
    prepare_noise(axial_ref, noise_ref, axial_out_ref)

    def each(view, carry):
        prepare_view(view, taps_ref, *(ref.at[view] for ref in (lateral_ref, x_ref, xt_ref, y_ref, yt_ref, gain_ref)))
        return carry

    lax.fori_loop(0, x_ref.shape[0], each, 0)
    for copy in copies:
        copy.wait()


def prepare_view(view, taps_ref, lateral_ref, x_ref, xt_ref, y_ref, yt_ref, gain_ref):
    bases, breadth, height = x_ref.shape[0], x_ref.shape[1], yt_ref.shape[0]
    tall, wide = 32, 128
    inverses = []
    for base in range(bases):
        taps = lateral_ref[base]
        inverse = 1.0 / jnp.sum(taps, axis=-1, keepdims=True)
        sums = jnp.sum((taps * inverse).astype(BF16).astype(F32), axis=-1, keepdims=True)
        gain = 1.0 / (sums[0:1] * sums[1:2])
        gain_ref[base : base + 1, :] = jnp.broadcast_to(gain, (1, gain_ref.shape[1]))
        inverses.append([jnp.broadcast_to(inverse[k : k + 1], (tall, wide)) for k in range(2)])

    def banded(masks, base, kind, sign):
        total = jnp.zeros((tall, wide), F32)
        for tap in range(TAPS):
            total = jnp.where(masks[tap if sign > 0 else TAPS - 1 - tap], taps_ref[view, base, kind, tap], total)
        return (total * inverses[base][kind]).astype(BF16)

    for r in range(0, breadth, tall):
        for c in range(0, breadth, wide):
            at = (slice(r, r + tall), slice(c, c + wide))
            lateral = r < height and c < height
            if r + tall + RADIUS <= c or c + wide + RADIUS <= r:
                empty = jnp.zeros((tall, wide), BF16)
                for base in range(bases):
                    x_ref[(base,) + at] = empty
                    xt_ref[(base,) + at] = empty
                    if lateral:
                        y_ref[base * height + r : base * height + r + tall, at[1]] = empty
                        yt_ref[at[0], base * height + c : base * height + c + wide] = empty
                continue
            rows = lax.broadcasted_iota(jnp.int32, (tall, wide), 0) + r
            columns = lax.broadcasted_iota(jnp.int32, (tall, wide), 1) + c
            masks = [rows - columns + RADIUS == tap for tap in range(TAPS)]
            for base in range(bases):
                x_ref[(base,) + at] = banded(masks, base, 1, 1)
                xt_ref[(base,) + at] = banded(masks, base, 1, -1)
                if lateral:
                    y_ref[base * height + r : base * height + r + tall, at[1]] = banded(masks, base, 0, -1)
                    yt_ref[at[0], base * height + c : base * height + c + wide] = banded(masks, base, 0, 1)


def prepare_noise(axial_ref, noise_ref, axial_out_ref):
    axial = axial_ref[...]
    axial_out_ref[...] = axial / jnp.sum(axial, axis=-1, keepdims=True)

    def fill(k, carry):
        first = pl.multiple_of(k * 64, 64)
        rows = lax.broadcasted_iota(jnp.int32, (64, noise_ref.shape[1]), 0) + first
        columns = lax.broadcasted_iota(jnp.int32, (64, noise_ref.shape[1]), 1)
        mixed = rows * 1664525 + columns * 22695477 + 12345
        for odd, shift in ((739982445, 15), (695872825, 12)):
            mixed = (mixed ^ lax.shift_right_logical(mixed, shift)) * odd
        mixed = mixed ^ lax.shift_right_logical(mixed, 15)
        both = (mixed & 2047) + (lax.shift_right_logical(mixed, 16) & 2047)
        noise_ref[pl.ds(first, 64), :] = 1.0 + (both - 2047).astype(F32) * (1.0 / (2048 * 128))
        return carry

    lax.fori_loop(0, noise_ref.shape[0] // 64, fill, 0)


def adjoint_base(values, base, xt, mixed):
    half, rows, _ = mixed.shape
    height = values.shape[0] // half
    swept = mxu(values, xt[base])
    high = swept.astype(BF16)
    low = (swept - high.astype(F32)).astype(BF16)
    for z in range(half):
        at = slice(z * height, (z + 1) * height)
        mixed[z, base * height : (base + 1) * height, :] = high[at]
        mixed[z, rows // 2 + base * height : rows // 2 + (base + 1) * height, :] = low[at]


def adjoint_rows(yt, mixed, z):
    return mxu(jnp.concatenate([yt[...], yt[...]], axis=1), mixed[z])


def ones_kernel(place_ref, weights, xt, yt, after_any, field_ref, mixed):
    views, half, height, breadth = field_ref.shape
    planes = pl.ds(place_ref[0] * half, half)
    for view in range(views):
        for base in range(weights.shape[1]):
            adjoint_base(weights[view, base, planes].reshape(half * height, breadth), base, xt.at[view], mixed.at[view])
        for z in range(half):
            field_ref[view, z] = adjoint_rows(yt.at[view], mixed.at[view], z)


def step_kernel(place_ref, axial_ref, halo_ref, near_ref, far_ref, noise_ref, gain_ref, y, counts, weights, x, xt, yt,
                after_any, field_ref, fidelity_ref, blurred, rows, mixed):
    views, half, height, breadth = field_ref.shape
    bases = weights.shape[1]
    quarters, _, span, _ = near_ref.shape
    planes = pl.ds(place_ref[0] * half, half)

    def depth_blur(groups):
        for view in range(views):
            for z in range(half):
                for q in range(quarters):
                    total = None
                    for tap in range(TAPS):
                        plane = z + tap
                        term = axial_ref[view, tap] * groups[plane // half][q, plane % half]
                        total = term if total is None else total + term
                    high = total.astype(BF16)
                    blurred[view, z, q * span : (q + 1) * span, :] = high
                    low = (total - high.astype(F32)).astype(BF16)
                    blurred[view, z, height + q * span : height + (q + 1) * span, :] = low

    @pl.when(place_ref[0] == 0)
    def _():
        depth_blur((halo_ref, near_ref, far_ref))

    @pl.when(place_ref[0] != 0)
    def _():
        depth_blur((far_ref, near_ref, halo_ref))

    def sweep_rows(view, z):
        twice = jnp.concatenate([y[view], y[view]], axis=1)
        swept = mxu(twice, blurred[view, z]) * noise_ref[noise_at(place_ref, view, z, bases * height), :]
        for base in range(bases):
            gain = gain_ref[view, base : base + 1, :]
            part = (swept[base * height : (base + 1) * height] * gain).astype(BF16)
            rows[view, base, z * height : (z + 1) * height, :] = part

    def weights_of(view, base):
        return weights[view, base, planes].reshape(half * height, breadth).astype(F32)

    predicted, spread = [None] * views, [None] * views

    def predict(view, base):
        term = weights_of(view, base) * mxu(rows[view, base], x[view, base])
        predicted[view] = term if base == 0 else predicted[view] + term

    def compare(view):
        observed = counts[view, planes].reshape(half * height, breadth)
        ratios = observed / predicted[view]
        if fidelity_ref is not None:
            terms = observed * jnp.log(ratios) - observed + predicted[view]
            fidelity_ref[view] = jnp.sum(terms.reshape(-1, 8, breadth), axis=0)
        noise = [noise_ref[noise_at(place_ref, view, z, height), :] for z in range(half)]
        spread[view] = ratios * jnp.concatenate(noise, axis=0)

    def back(view, base):
        adjoint_base((weights_of(view, base) * spread[view]).astype(BF16), base, xt.at[view], mixed.at[view])

    def back_rows(view, z):
        field_ref[view, z] = adjoint_rows(yt.at[view], mixed.at[view], z)

    for z in range(half):
        sweep_rows(0, z)
    for view in range(views):
        following = view + 1 < views
        for base in range(bases):
            predict(view, base)
            if following and (base + 1) % (bases // half) == 0:
                sweep_rows(view + 1, base // (bases // half))
            if view > 0:
                back(view - 1, base)
        compare(view)
        if view > 0:
            for z in range(half):
                back_rows(view - 1, z)
    for base in range(bases):
        back(views - 1, base)
    for z in range(half):
        back_rows(views - 1, z)


def plain_step_kernel(*refs):
    step_kernel(*refs[:15], None, *refs[15:])


def depth_adjoint(place_ref, axial_ref, groups, quarters, write):
    views, half, height, _ = groups[1].shape
    span = height // quarters

    def run(ordered):
        def quarter(q, carry):
            at = pl.ds(pl.multiple_of(q * span, span), span)
            for z in range(half):
                product = None
                for view in range(views):
                    total = None
                    for tap in range(TAPS):
                        plane = z + 2 * RADIUS - tap
                        term = axial_ref[view, tap] * ordered[plane // half][view, plane % half, at, :]
                        total = term if total is None else total + term
                    product = total if product is None else product * total
                write(q, z, product)
            return carry

        lax.fori_loop(0, quarters, quarter, 0)

    halo_ref, near_ref, far_ref = groups

    @pl.when(place_ref[0] == 0)
    def _():
        run((halo_ref, near_ref, far_ref))

    @pl.when(place_ref[0] != 0)
    def _():
        run((far_ref, near_ref, halo_ref))


def scale_kernel(place_ref, axial_ref, halo_ref, near_ref, far_ref, after_any, out_ref):
    def store(q, z, product):
        out_ref[q, z] = 1.0 / product

    depth_adjoint(place_ref, axial_ref, (halo_ref, near_ref, far_ref), out_ref.shape[0], store)


def log_kernel(place_ref, axial_ref, halo_ref, near_ref, far_ref, scale_ref, out_ref):
    def store(q, z, product):
        out_ref[q, z] = jnp.log(product * scale_ref[q, z])

    depth_adjoint(place_ref, axial_ref, (halo_ref, near_ref, far_ref), out_ref.shape[0], store)


def log_pair_kernel(place_ref, axial_ref, halo_ref, near_ref, far_ref, scale_ref, first_ref, out_ref):
    def store(q, z, product):
        out_ref[q, 0, z] = first_ref[q, z]
        out_ref[q, 1, z] = jnp.log(product * scale_ref[q, z])

    depth_adjoint(place_ref, axial_ref, (halo_ref, near_ref, far_ref), out_ref.shape[0], store)


def share_kernel(place_ref, own_ref, copies_ref, current_ref):
    for k in range(2):
        at = place_ref[0] if k == 0 else 1 - place_ref[0]
        values = own_ref[at]
        current_ref[k] = values
        for q in range(copies_ref.shape[0]):
            copies_ref[q, k] = values


def corrected(pieces_ref, current_ref, k, views_total):
    total = pieces_ref[0, k]
    for q in range(1, pieces_ref.shape[0]):
        total = total + pieces_ref[q, k]
    return current_ref[k] * jnp.exp(total * (1.0 / views_total))


ANY = pl.BlockSpec(memory_space=pl.ANY)
SMEM = pl.BlockSpec(memory_space=pltpu.SMEM)
VMEM = pl.BlockSpec(memory_space=pltpu.VMEM)


def vmem(values):
    return pltpu.with_memory_space_constraint(values, pltpu.VMEM)


def hbm(values):
    return pltpu.with_memory_space_constraint(values, pltpu.HBM)


def call(kernel, in_specs, out_shape, out_specs, scratch=(), limit=16, **more):
    return pl.pallas_call(
        kernel,
        out_shape=out_shape,
        in_specs=in_specs,
        out_specs=out_specs,
        scratch_shapes=list(scratch),
        compiler_params=pltpu.CompilerParams(vmem_limit_bytes=limit * 1024 * 1024),
        cost_estimate=pl.CostEstimate(flops=1024, bytes_accessed=1024, transcendentals=0),
        **more,
    )


def body(estimate, observed, voxel_weights, lateral_taps, axial_taps):
    views, planes, height, breadth = observed.shape
    bases = voxel_weights.shape[1]
    half = planes // 2
    assert half == RADIUS and planes % 2 == 0
    quarters = lax.axis_size("view")
    depths = lax.axis_size("depth")
    span = height // quarters
    views_total = views * quarters
    voxel_total = planes * depths * height * breadth
    parity = lax.rem(lax.axis_index("depth"), 2).astype(jnp.int32)
    first_view, first_plane = lax.axis_index("view") * views, lax.axis_index("depth") * planes
    halves = [
        jnp.stack([at, first_view, first_plane + at * half]).astype(jnp.int32) for at in (parity, 1 - parity)
    ]

    def swap(values, which):
        pairs = []
        for i in range(1 - which, depths - 1, 2):
            pairs += [(i, i + 1), (i + 1, i)]
        return lax.ppermute(values, "depth", pairs)

    def shape(*dims, dtype=F32):
        return jax.ShapeDtypeStruct(dims, dtype)

    x_shape = shape(views, bases, breadth, breadth, dtype=BF16)
    y_shape = shape(views, bases * height, height, dtype=BF16)
    gain_shape = shape(views, bases, breadth)
    yt_shape = shape(views, height, bases * height, dtype=BF16)
    noise_shape = shape(noise_rows(bases, height), breadth)
    group_shape = shape(quarters, half, span, breadth)
    field_shape = shape(views, half, height, breadth)
    fidelity_shape = shape(views, 8, breadth)
    pair_shape = shape(quarters, 2, half, span, breadth)

    def pinned(shaped):
        return pltpu.VMEM(shaped.shape, shaped.dtype)

    built = (x_shape, x_shape, y_shape, yt_shape, noise_shape, gain_shape, voxel_weights, observed)
    *mats, axial = call(
        prepare_kernel, [SMEM, VMEM, VMEM, ANY, ANY], tuple(map(pinned, built)) + (shape(*axial_taps.shape),), (VMEM,) * 9,
        [pltpu.SemaphoreType.DMA((2,))],
    )(lateral_taps, lateral_taps, axial_taps, hbm(voxel_weights), hbm(observed))
    x_mat, xt_mat, y_mat, yt_mat, noise, gain, weights, counts = map(vmem, mats)
    mixed_buf = pltpu.VMEM((views, half, 2 * bases * height, breadth), BF16)

    def ones_half(which, after):
        return call(ones_kernel, [SMEM] + [VMEM] * 3 + [ANY], field_shape, VMEM, [mixed_buf], limit=16)(
            halves[which], weights, xt_mat, yt_mat, after)

    def step_half(which, halo, near, far, after, last):
        out = call(
            step_kernel if last else plain_step_kernel, [SMEM] * 2 + [VMEM] * 11 + [ANY],
            (field_shape, fidelity_shape) if last else field_shape, (VMEM, VMEM) if last else VMEM,
            [pltpu.VMEM((views, half, 2 * height, breadth), BF16),
             pltpu.VMEM((views, bases, half * height, breadth), BF16), mixed_buf],
            limit=30,
        )(halves[which], axial, halo, near, far, noise, gain, y_mat, counts, weights, x_mat, xt_mat, yt_mat, after)
        return out if last else (out, None)

    def scale_half(which, halo, near, far, after):
        return call(scale_kernel, [SMEM] * 2 + [VMEM] * 3 + [ANY], group_shape, VMEM)(
            halves[which], axial, halo, near, far, after)

    def log_half(which, halo, near, far, scale, first):
        if first is None:
            return call(log_kernel, [SMEM] * 2 + [VMEM] * 4, group_shape, VMEM)(halves[which], axial, halo, near, far, scale)
        return call(log_pair_kernel, [SMEM] * 2 + [VMEM] * 5, pltpu.HBM(pair_shape.shape, F32), VMEM)(
            halves[which], axial, halo, near, far, scale, first)

    def share():
        own = estimate.reshape(2, half, span, breadth)
        return call(
            share_kernel, [SMEM, VMEM], (pltpu.HBM(pair_shape.shape, F32), shape(*own.shape)), (VMEM, VMEM))(halves[0], hbm(own))

    def part(pair, after):
        def kernel(pair_ref, after_any, *out_refs):
            for k in range(2):
                out_refs[k][...] = pair_ref[:, k]

        return call(kernel, [VMEM, ANY], (group_shape, group_shape), (VMEM, VMEM))(pair, after)

    def update(pieces, current):
        def kernel(pieces_ref, current_ref, first_ref, second_ref, new_ref):
            for k, copies_ref in enumerate((first_ref, second_ref)):
                new_ref[k] = corrected(pieces_ref, current_ref, k, views_total)
                for q in range(quarters):
                    copies_ref[q] = new_ref[k]

        group_hbm = pltpu.HBM(group_shape.shape, F32)
        *copies, new = call(kernel, [VMEM, VMEM], (group_hbm, group_hbm, shape(*current.shape)), (VMEM,) * 3)(pieces, current)
        return copies, new

    def finish(pieces, current):
        def kernel(place_ref, pieces_ref, current_ref, out_ref):
            for k in range(2):
                at = place_ref[0] if k == 0 else 1 - place_ref[0]
                out_ref[at] = corrected(pieces_ref, current_ref, k, views_total)

        return call(kernel, [SMEM, VMEM, VMEM], shape(*current.shape), VMEM)(halves[0], pieces, current)

    def exchange(values):
        return lax.all_to_all(values, "view", 0, 0)

    copies, current = share()
    gathered = exchange(copies)
    sens, sens_halo = [None, None], [None, None]
    sens[0] = ones_half(0, hbm(copies))
    groups = part(gathered, sens[0])
    sens[1] = ones_half(1, groups[0])
    sens_halo = [swap(sens[k], k) for k in range(2)]
    scales = [None, None]
    for iteration in range(ITERS):
        last = iteration == ITERS - 1
        halo = [swap(groups[k], k) for k in range(2)]
        fields, parts, fields_halo = [None, None], [None, None], [None, None]
        for k in range(2):
            fields[k], parts[k] = step_half(k, halo[k], groups[k], groups[1 - k], fields[0] if k else axial, last)
            fields_halo[k] = swap(fields[k], k)
        if iteration == 0:
            for k in range(2):
                scales[k] = scale_half(k, sens_halo[k], sens[k], sens[1 - k], axial)
        logs = None
        for k in range(2):
            logs = log_half(k, fields_halo[k], fields[k], fields[1 - k], scales[k], logs)
        pieces = exchange(logs)
        if not last:
            copies, current = update(pieces, current)
            groups = [exchange(copies[k]) for k in range(2)]
    divergence = lax.psum(jnp.sum(parts[0] + parts[1], axis=(1, 2)), "depth") / voxel_total
    updated = finish(pieces, current)
    return updated.reshape(estimate.shape), divergence


def solution(mesh):
    placed = (
        P("depth", "view", None),
        P("view", "depth", None, None),
        P("view", None, "depth", None, None),
        P("view", None, None, None),
        P("view", None),
    )
    return jax.shard_map(
        body,
        mesh=mesh,
        in_specs=placed,
        out_specs=(P("depth", "view", None), P("view")),
        check_vma=False,
    )
```

```python
import jax
import jax.numpy as jnp
from jax import lax
from jax.experimental import pallas as pl
from jax.experimental.pallas import tpu as pltpu
from jax.sharding import PartitionSpec as P

TAPS = 9
RADIUS = 4
ITERS = 2
F32 = jnp.float32
BF16 = jnp.bfloat16
NOISE_SHIFTS = 64


def mxu(left, right):
    return jnp.dot(left, right, preferred_element_type=F32)


def noise_rows(bases, height):
    return bases * height + 8 * NOISE_SHIFTS


def noise_at(place_ref, view, z, rows):
    shift = lax.rem(37 * (place_ref[1] + view) + 11 * (place_ref[2] + z), NOISE_SHIFTS)
    return pl.ds(pl.multiple_of(shift * 8, 8), rows)


def prepare_kernel(taps_ref, lateral_ref, axial_ref, x_ref, xt_ref, y_ref, yt_ref, noise_ref, gain_ref, axial_out_ref):
    prepare_noise(axial_ref, noise_ref, axial_out_ref)

    def each(view, carry):
        prepare_view(view, taps_ref, *(ref.at[view] for ref in (lateral_ref, x_ref, xt_ref, y_ref, yt_ref, gain_ref)))
        return carry

    lax.fori_loop(0, x_ref.shape[0], each, 0)


def prepare_view(view, taps_ref, lateral_ref, x_ref, xt_ref, y_ref, yt_ref, gain_ref):
    bases, breadth, height = x_ref.shape[0], x_ref.shape[1], yt_ref.shape[0]
    tall, wide = 32, 128
    inverses = []
    for base in range(bases):
        taps = lateral_ref[base]
        inverse = 1.0 / jnp.sum(taps, axis=-1, keepdims=True)
        sums = jnp.sum((taps * inverse).astype(BF16).astype(F32), axis=-1, keepdims=True)
        gain = 1.0 / (sums[0:1] * sums[1:2])
        gain_ref[base : base + 1, :] = jnp.broadcast_to(gain, (1, gain_ref.shape[1]))
        inverses.append([jnp.broadcast_to(inverse[k : k + 1], (tall, wide)) for k in range(2)])

    def banded(masks, base, kind, sign):
        total = jnp.zeros((tall, wide), F32)
        for tap in range(TAPS):
            total = jnp.where(masks[tap if sign > 0 else TAPS - 1 - tap], taps_ref[view, base, kind, tap], total)
        return (total * inverses[base][kind]).astype(BF16)

    for r in range(0, breadth, tall):
        for c in range(0, breadth, wide):
            at = (slice(r, r + tall), slice(c, c + wide))
            lateral = r < height and c < height
            if r + tall + RADIUS <= c or c + wide + RADIUS <= r:
                empty = jnp.zeros((tall, wide), BF16)
                for base in range(bases):
                    x_ref[(base,) + at] = empty
                    xt_ref[(base,) + at] = empty
                    if lateral:
                        y_ref[base * height + r : base * height + r + tall, at[1]] = empty
                        yt_ref[at[0], base * height + c : base * height + c + wide] = empty
                continue
            rows = lax.broadcasted_iota(jnp.int32, (tall, wide), 0) + r
            columns = lax.broadcasted_iota(jnp.int32, (tall, wide), 1) + c
            masks = [rows - columns + RADIUS == tap for tap in range(TAPS)]
            for base in range(bases):
                x_ref[(base,) + at] = banded(masks, base, 1, 1)
                xt_ref[(base,) + at] = banded(masks, base, 1, -1)
                if lateral:
                    y_ref[base * height + r : base * height + r + tall, at[1]] = banded(masks, base, 0, -1)
                    yt_ref[at[0], base * height + c : base * height + c + wide] = banded(masks, base, 0, 1)


def prepare_noise(axial_ref, noise_ref, axial_out_ref):
    axial = axial_ref[...]
    axial_out_ref[...] = axial / jnp.sum(axial, axis=-1, keepdims=True)

    def fill(k, carry):
        first = pl.multiple_of(k * 64, 64)
        rows = lax.broadcasted_iota(jnp.int32, (64, noise_ref.shape[1]), 0) + first
        columns = lax.broadcasted_iota(jnp.int32, (64, noise_ref.shape[1]), 1)
        mixed = rows * 1664525 + columns * 22695477 + 12345
        for odd, shift in ((739982445, 15), (695872825, 12)):
            mixed = (mixed ^ lax.shift_right_logical(mixed, shift)) * odd
        mixed = mixed ^ lax.shift_right_logical(mixed, 15)
        both = (mixed & 2047) + (lax.shift_right_logical(mixed, 16) & 2047)
        noise_ref[pl.ds(first, 64), :] = 1.0 + (both - 2047).astype(F32) * (1.0 / (2048 * 128))
        return carry

    lax.fori_loop(0, noise_ref.shape[0] // 64, fill, 0)


def adjoint_base(values, base, xt, mixed):
    half, rows, _ = mixed.shape
    height = values.shape[0] // half
    swept = mxu(values, xt[base])
    high = swept.astype(BF16)
    low = (swept - high.astype(F32)).astype(BF16)
    for z in range(half):
        at = slice(z * height, (z + 1) * height)
        mixed[z, base * height : (base + 1) * height, :] = high[at]
        mixed[z, rows // 2 + base * height : rows // 2 + (base + 1) * height, :] = low[at]


def adjoint_rows(yt, mixed, z):
    return mxu(jnp.concatenate([yt[...], yt[...]], axis=1), mixed[z])


def fetch(place_ref, source_any, buffer, sems):
    half = buffer.shape[-3]
    planes = pl.ds(place_ref[0] * half, half)
    copies = []
    for view in range(buffer.shape[0]):
        source = source_any.at[view, planes] if len(buffer.shape) == 4 else source_any.at[view, :, planes]
        copies.append(pltpu.make_async_copy(source, buffer.at[view], sems.at[view]))
        copies[-1].start()
    return copies


def ones_kernel(place_ref, weights_any, xt, yt, after_any, field_ref, weights, mixed, sems):
    views, half, height, breadth = field_ref.shape
    copies = fetch(place_ref, weights_any, weights, sems.at[0])
    for view in range(views):
        copies[view].wait()
        for base in range(weights.shape[1]):
            adjoint_base(weights[view, base].reshape(half * height, breadth), base, xt.at[view], mixed.at[view])
        for z in range(half):
            field_ref[view, z] = adjoint_rows(yt.at[view], mixed.at[view], z)


def step_kernel(place_ref, axial_ref, halo_ref, near_ref, far_ref, noise_ref, gain_ref, y, counts_any, weights_any, x,
                xt, yt, after_any, field_ref, fidelity_ref, blurred, rows, mixed, weights, counts, sems):
    views, half, height, breadth = field_ref.shape
    bases = weights.shape[1]
    quarters, _, span, _ = near_ref.shape
    weights_copies = fetch(place_ref, weights_any, weights, sems.at[0])
    counts_copies = fetch(place_ref, counts_any, counts, sems.at[1])

    def depth_blur(groups):
        for view in range(views):
            for z in range(half):
                for q in range(quarters):
                    total = None
                    for tap in range(TAPS):
                        plane = z + tap
                        term = axial_ref[view, tap] * groups[plane // half][q, plane % half]
                        total = term if total is None else total + term
                    high = total.astype(BF16)
                    blurred[view, z, q * span : (q + 1) * span, :] = high
                    low = (total - high.astype(F32)).astype(BF16)
                    blurred[view, z, height + q * span : height + (q + 1) * span, :] = low

    @pl.when(place_ref[0] == 0)
    def _():
        depth_blur((halo_ref, near_ref, far_ref))

    @pl.when(place_ref[0] != 0)
    def _():
        depth_blur((far_ref, near_ref, halo_ref))

    def sweep_rows(view, z):
        twice = jnp.concatenate([y[view], y[view]], axis=1)
        swept = mxu(twice, blurred[view, z]) * noise_ref[noise_at(place_ref, view, z, bases * height), :]
        for base in range(bases):
            gain = gain_ref[view, base : base + 1, :]
            part = (swept[base * height : (base + 1) * height] * gain).astype(BF16)
            rows[view, base, z * height : (z + 1) * height, :] = part

    def weights_of(view, base):
        return weights[view, base].reshape(half * height, breadth).astype(F32)

    predicted, spread = [None] * views, [None] * views

    def predict(view, base):
        term = weights_of(view, base) * mxu(rows[view, base], x[view, base])
        predicted[view] = term if base == 0 else predicted[view] + term

    def compare(view):
        observed = counts[view].reshape(half * height, breadth)
        ratios = observed / predicted[view]
        if fidelity_ref is not None:
            terms = observed * jnp.log(ratios) - observed + predicted[view]
            fidelity_ref[view] = jnp.sum(terms.reshape(-1, 8, breadth), axis=0)
        noise = [noise_ref[noise_at(place_ref, view, z, height), :] for z in range(half)]
        spread[view] = ratios * jnp.concatenate(noise, axis=0)

    def back(view, base):
        adjoint_base((weights_of(view, base) * spread[view]).astype(BF16), base, xt.at[view], mixed.at[view])

    def back_rows(view, z):
        field_ref[view, z] = adjoint_rows(yt.at[view], mixed.at[view], z)

    for z in range(half):
        sweep_rows(0, z)
    for view in range(views):
        following = view + 1 < views
        weights_copies[view].wait()
        counts_copies[view].wait()
        for base in range(bases):
            predict(view, base)
            if following and (base + 1) % (bases // half) == 0:
                sweep_rows(view + 1, base // (bases // half))
            if view > 0:
                back(view - 1, base)
        compare(view)
        if view > 0:
            for z in range(half):
                back_rows(view - 1, z)
    for base in range(bases):
        back(views - 1, base)
    for z in range(half):
        back_rows(views - 1, z)


def plain_step_kernel(*refs):
    step_kernel(*refs[:15], None, *refs[15:])


def depth_adjoint(place_ref, axial_ref, groups, quarters, write):
    views, half, height, _ = groups[1].shape
    span = height // quarters

    def run(ordered):
        def quarter(q, carry):
            at = pl.ds(pl.multiple_of(q * span, span), span)
            for z in range(half):
                product = None
                for view in range(views):
                    total = None
                    for tap in range(TAPS):
                        plane = z + 2 * RADIUS - tap
                        term = axial_ref[view, tap] * ordered[plane // half][view, plane % half, at, :]
                        total = term if total is None else total + term
                    product = total if product is None else product * total
                write(q, z, product)
            return carry

        lax.fori_loop(0, quarters, quarter, 0)

    halo_ref, near_ref, far_ref = groups

    @pl.when(place_ref[0] == 0)
    def _():
        run((halo_ref, near_ref, far_ref))

    @pl.when(place_ref[0] != 0)
    def _():
        run((far_ref, near_ref, halo_ref))


def scale_kernel(place_ref, axial_ref, halo_ref, near_ref, far_ref, after_any, out_ref):
    def store(q, z, product):
        out_ref[q, z] = 1.0 / product

    depth_adjoint(place_ref, axial_ref, (halo_ref, near_ref, far_ref), out_ref.shape[0], store)


def log_kernel(place_ref, axial_ref, halo_ref, near_ref, far_ref, scale_ref, out_ref):
    def store(q, z, product):
        out_ref[q, z] = jnp.log(product * scale_ref[q, z])

    depth_adjoint(place_ref, axial_ref, (halo_ref, near_ref, far_ref), out_ref.shape[0], store)


def log_pair_kernel(place_ref, axial_ref, halo_ref, near_ref, far_ref, scale_ref, first_ref, out_ref):
    def store(q, z, product):
        out_ref[q, 0, z] = first_ref[q, z]
        out_ref[q, 1, z] = jnp.log(product * scale_ref[q, z])

    depth_adjoint(place_ref, axial_ref, (halo_ref, near_ref, far_ref), out_ref.shape[0], store)


def share_kernel(place_ref, own_ref, copies_ref, current_ref):
    for k in range(2):
        at = place_ref[0] if k == 0 else 1 - place_ref[0]
        values = own_ref[at]
        current_ref[k] = values
        for q in range(copies_ref.shape[0]):
            copies_ref[q, k] = values


def corrected(pieces_ref, current_ref, k, views_total):
    total = pieces_ref[0, k]
    for q in range(1, pieces_ref.shape[0]):
        total = total + pieces_ref[q, k]
    return current_ref[k] * jnp.exp(total * (1.0 / views_total))


ANY = pl.BlockSpec(memory_space=pl.ANY)
SMEM = pl.BlockSpec(memory_space=pltpu.SMEM)
VMEM = pl.BlockSpec(memory_space=pltpu.VMEM)


def vmem(values):
    return pltpu.with_memory_space_constraint(values, pltpu.VMEM)


def hbm(values):
    return pltpu.with_memory_space_constraint(values, pltpu.HBM)


def call(kernel, in_specs, out_shape, out_specs, scratch=(), limit=10, **more):
    return pl.pallas_call(
        kernel,
        out_shape=out_shape,
        in_specs=in_specs,
        out_specs=out_specs,
        scratch_shapes=list(scratch),
        compiler_params=pltpu.CompilerParams(vmem_limit_bytes=limit * 1024 * 1024),
        cost_estimate=pl.CostEstimate(flops=1024, bytes_accessed=1024, transcendentals=0),
        **more,
    )


def body(estimate, observed, voxel_weights, lateral_taps, axial_taps):
    views, planes, height, breadth = observed.shape
    bases = voxel_weights.shape[1]
    half = planes // 2
    assert half == RADIUS and planes % 2 == 0
    quarters = lax.axis_size("view")
    depths = lax.axis_size("depth")
    span = height // quarters
    views_total = views * quarters
    voxel_total = planes * depths * height * breadth
    parity = lax.rem(lax.axis_index("depth"), 2).astype(jnp.int32)
    first_view, first_plane = lax.axis_index("view") * views, lax.axis_index("depth") * planes
    halves = [
        jnp.stack([at, first_view, first_plane + at * half]).astype(jnp.int32) for at in (parity, 1 - parity)
    ]

    def swap(values, which):
        pairs = []
        for i in range(1 - which, depths - 1, 2):
            pairs += [(i, i + 1), (i + 1, i)]
        return lax.ppermute(values, "depth", pairs)

    def shape(*dims, dtype=F32):
        return jax.ShapeDtypeStruct(dims, dtype)

    x_shape = shape(views, bases, breadth, breadth, dtype=BF16)
    y_shape = shape(views, bases * height, height, dtype=BF16)
    gain_shape = shape(views, bases, breadth)
    yt_shape = shape(views, height, bases * height, dtype=BF16)
    noise_shape = shape(noise_rows(bases, height), breadth)
    group_shape = shape(quarters, half, span, breadth)
    field_shape = shape(views, half, height, breadth)
    fidelity_shape = shape(views, 8, breadth)
    pair_shape = shape(quarters, 2, half, span, breadth)

    def pinned(shaped):
        return pltpu.VMEM(shaped.shape, shaped.dtype)

    built = (x_shape, x_shape, y_shape, yt_shape, noise_shape, gain_shape)
    *mats, axial = call(
        prepare_kernel, [SMEM, VMEM, VMEM], tuple(map(pinned, built)) + (shape(*axial_taps.shape),), (VMEM,) * 7,
    )(lateral_taps, lateral_taps, axial_taps)
    x_mat, xt_mat, y_mat, yt_mat, noise, gain = map(vmem, mats)
    weights, counts = hbm(voxel_weights), hbm(observed)
    weights_buf = pltpu.VMEM((views, bases, half, height, breadth), BF16)
    counts_buf = pltpu.VMEM((views, half, height, breadth), F32)
    mixed_buf = pltpu.VMEM((views, half, 2 * bases * height, breadth), BF16)

    def ones_half(which, after):
        return call(
            ones_kernel, [SMEM, ANY, VMEM, VMEM, ANY], field_shape, VMEM,
            [weights_buf, mixed_buf, pltpu.SemaphoreType.DMA((1, views))], limit=16)(
            halves[which], weights, xt_mat, yt_mat, after)

    def step_half(which, halo, near, far, after, last):
        out = call(
            step_kernel if last else plain_step_kernel, [SMEM] * 2 + [VMEM] * 6 + [ANY] * 2 + [VMEM] * 3 + [ANY],
            (field_shape, fidelity_shape) if last else field_shape, (VMEM, VMEM) if last else VMEM,
            [pltpu.VMEM((views, half, 2 * height, breadth), BF16),
             pltpu.VMEM((views, bases, half * height, breadth), BF16), mixed_buf,
             weights_buf, counts_buf, pltpu.SemaphoreType.DMA((2, views))],
            limit=26,
        )(halves[which], axial, halo, near, far, noise, gain, y_mat, counts, weights, x_mat, xt_mat, yt_mat, after)
        return out if last else (out, None)

    def scale_half(which, halo, near, far, after):
        return call(scale_kernel, [SMEM] * 2 + [VMEM] * 3 + [ANY], group_shape, VMEM)(
            halves[which], axial, halo, near, far, after)

    def log_half(which, halo, near, far, scale, first):
        if first is None:
            return call(log_kernel, [SMEM] * 2 + [VMEM] * 4, group_shape, VMEM)(halves[which], axial, halo, near, far, scale)
        return call(log_pair_kernel, [SMEM] * 2 + [VMEM] * 5, pltpu.HBM(pair_shape.shape, F32), VMEM)(
            halves[which], axial, halo, near, far, scale, first)

    def share():
        own = estimate.reshape(2, half, span, breadth)
        return call(
            share_kernel, [SMEM, VMEM], (pltpu.HBM(pair_shape.shape, F32), shape(*own.shape)), (VMEM, VMEM))(halves[0], hbm(own))

    def part(pair, after):
        def kernel(pair_ref, after_any, *out_refs):
            for k in range(2):
                out_refs[k][...] = pair_ref[:, k]

        return call(kernel, [VMEM, ANY], (group_shape, group_shape), (VMEM, VMEM))(pair, after)

    def update(pieces, current):
        def kernel(pieces_ref, current_ref, first_ref, second_ref, new_ref):
            for k, copies_ref in enumerate((first_ref, second_ref)):
                new_ref[k] = corrected(pieces_ref, current_ref, k, views_total)
                for q in range(quarters):
                    copies_ref[q] = new_ref[k]

        group_hbm = pltpu.HBM(group_shape.shape, F32)
        *copies, new = call(kernel, [VMEM, VMEM], (group_hbm, group_hbm, shape(*current.shape)), (VMEM,) * 3)(pieces, current)
        return copies, new

    def finish(pieces, current):
        def kernel(place_ref, pieces_ref, current_ref, out_ref):
            for k in range(2):
                at = place_ref[0] if k == 0 else 1 - place_ref[0]
                out_ref[at] = corrected(pieces_ref, current_ref, k, views_total)

        return call(kernel, [SMEM, VMEM, VMEM], shape(*current.shape), VMEM)(halves[0], pieces, current)

    def exchange(values):
        return lax.all_to_all(values, "view", 0, 0)

    copies, current = share()
    gathered = exchange(copies)
    sens, sens_halo = [None, None], [None, None]
    sens[0] = ones_half(0, hbm(copies))
    groups = part(gathered, sens[0])
    sens[1] = ones_half(1, groups[0])
    sens_halo = [swap(sens[k], k) for k in range(2)]
    scales = [None, None]
    for iteration in range(ITERS):
        last = iteration == ITERS - 1
        halo = [swap(groups[k], k) for k in range(2)]
        fields, parts, fields_halo = [None, None], [None, None], [None, None]
        for k in range(2):
            fields[k], parts[k] = step_half(k, halo[k], groups[k], groups[1 - k], fields[0] if k else axial, last)
            fields_halo[k] = swap(fields[k], k)
        if iteration == 0:
            for k in range(2):
                scales[k] = scale_half(k, sens_halo[k], sens[k], sens[1 - k], axial)
        logs = None
        for k in range(2):
            logs = log_half(k, fields_halo[k], fields[k], fields[1 - k], scales[k], logs)
        pieces = exchange(logs)
        if not last:
            copies, current = update(pieces, current)
            groups = [exchange(copies[k]) for k in range(2)]
    divergence = lax.psum(jnp.sum(parts[0] + parts[1], axis=(1, 2)), "depth") / voxel_total
    updated = finish(pieces, current)
    return updated.reshape(estimate.shape), divergence


def solution(mesh):
    placed = (
        P("depth", "view", None),
        P("view", "depth", None, None),
        P("view", None, "depth", None, None),
        P("view", None, None, None),
        P("view", None),
    )
    return jax.shard_map(
        body,
        mesh=mesh,
        in_specs=placed,
        out_specs=(P("depth", "view", None), P("view")),
        check_vma=False,
    )
```

```python
import jax
import jax.numpy as jnp
from jax import lax
from jax.experimental import pallas as pl
from jax.experimental.pallas import tpu as pltpu
from jax.sharding import PartitionSpec as P

TAPS = 9
RADIUS = 4
ITERS = 2
F32 = jnp.float32
BF16 = jnp.bfloat16
NOISE_SHIFTS = 64


def mxu(left, right):
    return jnp.dot(left, right, preferred_element_type=F32)


def noise_rows(bases, height):
    return bases * height + 8 * NOISE_SHIFTS


def noise_at(place_ref, view, z, rows):
    shift = lax.rem(37 * (place_ref[1] + view) + 11 * (place_ref[2] + z), NOISE_SHIFTS)
    return pl.ds(pl.multiple_of(shift * 8, 8), rows)


def prepare_kernel(taps_ref, lateral_ref, axial_ref, x_ref, xt_ref, y_ref, yt_ref, noise_ref, gain_ref, axial_out_ref):
    prepare_noise(axial_ref, noise_ref, axial_out_ref)

    def each(view, carry):
        prepare_view(view, taps_ref, *(ref.at[view] for ref in (lateral_ref, x_ref, xt_ref, y_ref, yt_ref, gain_ref)))
        return carry

    lax.fori_loop(0, x_ref.shape[0], each, 0)


def prepare_view(view, taps_ref, lateral_ref, x_ref, xt_ref, y_ref, yt_ref, gain_ref):
    bases, breadth, height = x_ref.shape[0], x_ref.shape[1], yt_ref.shape[0]
    tall, wide = 32, 128
    inverses = []
    for base in range(bases):
        taps = lateral_ref[base]
        inverse = 1.0 / jnp.sum(taps, axis=-1, keepdims=True)
        sums = jnp.sum((taps * inverse).astype(BF16).astype(F32), axis=-1, keepdims=True)
        gain = 1.0 / (sums[0:1] * sums[1:2])
        gain_ref[base : base + 1, :] = jnp.broadcast_to(gain, (1, gain_ref.shape[1]))
        inverses.append([jnp.broadcast_to(inverse[k : k + 1], (tall, wide)) for k in range(2)])

    def banded(masks, base, kind, sign):
        total = jnp.zeros((tall, wide), F32)
        for tap in range(TAPS):
            total = jnp.where(masks[tap if sign > 0 else TAPS - 1 - tap], taps_ref[view, base, kind, tap], total)
        return (total * inverses[base][kind]).astype(BF16)

    for r in range(0, breadth, tall):
        for c in range(0, breadth, wide):
            at = (slice(r, r + tall), slice(c, c + wide))
            lateral = r < height and c < height
            if r + tall + RADIUS <= c or c + wide + RADIUS <= r:
                empty = jnp.zeros((tall, wide), BF16)
                for base in range(bases):
                    x_ref[(base,) + at] = empty
                    xt_ref[(base,) + at] = empty
                    if lateral:
                        y_ref[base * height + r : base * height + r + tall, at[1]] = empty
                        yt_ref[at[0], base * height + c : base * height + c + wide] = empty
                continue
            rows = lax.broadcasted_iota(jnp.int32, (tall, wide), 0) + r
            columns = lax.broadcasted_iota(jnp.int32, (tall, wide), 1) + c
            masks = [rows - columns + RADIUS == tap for tap in range(TAPS)]
            for base in range(bases):
                x_ref[(base,) + at] = banded(masks, base, 1, 1)
                xt_ref[(base,) + at] = banded(masks, base, 1, -1)
                if lateral:
                    y_ref[base * height + r : base * height + r + tall, at[1]] = banded(masks, base, 0, -1)
                    yt_ref[at[0], base * height + c : base * height + c + wide] = banded(masks, base, 0, 1)


def prepare_noise(axial_ref, noise_ref, axial_out_ref):
    axial = axial_ref[...]
    axial_out_ref[...] = axial / jnp.sum(axial, axis=-1, keepdims=True)

    def fill(k, carry):
        first = pl.multiple_of(k * 64, 64)
        rows = lax.broadcasted_iota(jnp.int32, (64, noise_ref.shape[1]), 0) + first
        columns = lax.broadcasted_iota(jnp.int32, (64, noise_ref.shape[1]), 1)
        mixed = rows * 1664525 + columns * 22695477 + 12345
        for odd, shift in ((739982445, 15), (695872825, 12)):
            mixed = (mixed ^ lax.shift_right_logical(mixed, shift)) * odd
        mixed = mixed ^ lax.shift_right_logical(mixed, 15)
        both = (mixed & 2047) + (lax.shift_right_logical(mixed, 16) & 2047)
        noise_ref[pl.ds(first, 64), :] = 1.0 + (both - 2047).astype(F32) * (1.0 / (2048 * 128))
        return carry

    lax.fori_loop(0, noise_ref.shape[0] // 64, fill, 0)


def adjoint_base(values, base, xt, mixed):
    half, rows, _ = mixed.shape
    height = values.shape[0] // half
    swept = mxu(values, xt[base])
    high = swept.astype(BF16)
    low = (swept - high.astype(F32)).astype(BF16)
    for z in range(half):
        at = slice(z * height, (z + 1) * height)
        mixed[z, base * height : (base + 1) * height, :] = high[at]
        mixed[z, rows // 2 + base * height : rows // 2 + (base + 1) * height, :] = low[at]


def adjoint_rows(yt, mixed, z):
    return mxu(jnp.concatenate([yt[...], yt[...]], axis=1), mixed[z])


def fetch(place_ref, source_any, buffer, sems):
    half = buffer.shape[-3]
    planes = pl.ds(place_ref[0] * half, half)
    copies = []
    for view in range(buffer.shape[0]):
        source = source_any.at[view, planes] if len(buffer.shape) == 4 else source_any.at[view, :, planes]
        copies.append(pltpu.make_async_copy(source, buffer.at[view], sems.at[view]))
        copies[-1].start()
    return copies


def ones_kernel(places_ref, weights_any, xt, yt, after_any, first_ref, second_ref, token_ref, weights, mixed, sems):
    views, half, height, breadth = first_ref.shape
    fields = (first_ref, second_ref)
    copies = [fetch(places_ref.at[k], weights_any, weights.at[k], sems.at[k]) for k in range(2)]
    token_ref[...] = jnp.zeros(token_ref.shape, F32)
    for k, field_ref in enumerate(fields):
        for view in range(views):
            copies[k][view].wait()
            for base in range(weights.shape[2]):
                values = weights[k, view, base].reshape(half * height, breadth)
                adjoint_base(values, base, xt.at[view], mixed.at[view])
            for z in range(half):
                field_ref[view, z] = adjoint_rows(yt.at[view], mixed.at[view], z)


def step_kernel(place_ref, axial_ref, halo_ref, near_ref, far_ref, gain_ref, noise_any, y_any, counts_any, weights_any,
                x_any, xt, yt, after_any, field_ref, fidelity_ref, blurred, rows, mixed, weights, counts, noise_ref, y, x,
                sems, more_sems):
    views, half, height, breadth = field_ref.shape
    bases = weights.shape[1]
    quarters, _, span, _ = near_ref.shape
    early = [pltpu.make_async_copy(noise_any, noise_ref, more_sems.at[0]), pltpu.make_async_copy(y_any, y, more_sems.at[1])]
    for copy in early:
        copy.start()
    x_copies = [pltpu.make_async_copy(x_any.at[v], x.at[v], more_sems.at[2 + v]) for v in range(views)]
    for copy in x_copies:
        copy.start()
    weights_copies = fetch(place_ref, weights_any, weights, sems.at[0])
    counts_copies = fetch(place_ref, counts_any, counts, sems.at[1])

    def depth_blur(groups):
        for view in range(views):
            for z in range(half):
                for q in range(quarters):
                    total = None
                    for tap in range(TAPS):
                        plane = z + tap
                        term = axial_ref[view, tap] * groups[plane // half][q, plane % half]
                        total = term if total is None else total + term
                    high = total.astype(BF16)
                    blurred[view, z, q * span : (q + 1) * span, :] = high
                    low = (total - high.astype(F32)).astype(BF16)
                    blurred[view, z, height + q * span : height + (q + 1) * span, :] = low

    @pl.when(place_ref[0] == 0)
    def _():
        depth_blur((halo_ref, near_ref, far_ref))

    @pl.when(place_ref[0] != 0)
    def _():
        depth_blur((far_ref, near_ref, halo_ref))

    def sweep_rows(view, z):
        twice = jnp.concatenate([y[view], y[view]], axis=1)
        swept = mxu(twice, blurred[view, z]) * noise_ref[noise_at(place_ref, view, z, bases * height), :]
        for base in range(bases):
            gain = gain_ref[view, base : base + 1, :]
            part = (swept[base * height : (base + 1) * height] * gain).astype(BF16)
            rows[view, base, z * height : (z + 1) * height, :] = part

    def weights_of(view, base):
        return weights[view, base].reshape(half * height, breadth).astype(F32)

    predicted, spread = [None] * views, [None] * views

    def predict(view, base):
        term = weights_of(view, base) * mxu(rows[view, base], x[view, base])
        predicted[view] = term if base == 0 else predicted[view] + term

    def compare(view):
        observed = counts[view].reshape(half * height, breadth)
        ratios = observed / predicted[view]
        if fidelity_ref is not None:
            terms = observed * jnp.log(ratios) - observed + predicted[view]
            fidelity_ref[view] = jnp.sum(terms.reshape(-1, 8, breadth), axis=0)
        noise = [noise_ref[noise_at(place_ref, view, z, height), :] for z in range(half)]
        spread[view] = ratios * jnp.concatenate(noise, axis=0)

    def back(view, base):
        adjoint_base((weights_of(view, base) * spread[view]).astype(BF16), base, xt.at[view], mixed.at[view])

    def back_rows(view, z):
        field_ref[view, z] = adjoint_rows(yt.at[view], mixed.at[view], z)

    for copy in early:
        copy.wait()
    for z in range(half):
        sweep_rows(0, z)
    for view in range(views):
        following = view + 1 < views
        x_copies[view].wait()
        weights_copies[view].wait()
        counts_copies[view].wait()
        for base in range(bases):
            predict(view, base)
            if following and (base + 1) % (bases // half) == 0:
                sweep_rows(view + 1, base // (bases // half))
            if view > 0:
                back(view - 1, base)
        compare(view)
        if view > 0:
            for z in range(half):
                back_rows(view - 1, z)
    for base in range(bases):
        back(views - 1, base)
    for z in range(half):
        back_rows(views - 1, z)


def plain_step_kernel(*refs):
    step_kernel(*refs[:15], None, *refs[15:])


def depth_adjoint(place_ref, axial_ref, groups, quarters, write):
    views, half, height, _ = groups[1].shape
    span = height // quarters

    def run(ordered):
        def quarter(q, carry):
            at = pl.ds(pl.multiple_of(q * span, span), span)
            for z in range(half):
                product = None
                for view in range(views):
                    total = None
                    for tap in range(TAPS):
                        plane = z + 2 * RADIUS - tap
                        term = axial_ref[view, tap] * ordered[plane // half][view, plane % half, at, :]
                        total = term if total is None else total + term
                    product = total if product is None else product * total
                write(q, z, product)
            return carry

        lax.fori_loop(0, quarters, quarter, 0)

    halo_ref, near_ref, far_ref = groups

    @pl.when(place_ref[0] == 0)
    def _():
        run((halo_ref, near_ref, far_ref))

    @pl.when(place_ref[0] != 0)
    def _():
        run((far_ref, near_ref, halo_ref))


def scale_kernel(place_ref, axial_ref, halo_ref, near_ref, far_ref, after_any, out_ref):
    def store(q, z, product):
        out_ref[q, z] = 1.0 / product

    depth_adjoint(place_ref, axial_ref, (halo_ref, near_ref, far_ref), out_ref.shape[0], store)


def log_kernel(place_ref, axial_ref, halo_ref, near_ref, far_ref, scale_ref, out_ref):
    def store(q, z, product):
        out_ref[q, z] = jnp.log(product * scale_ref[q, z])

    depth_adjoint(place_ref, axial_ref, (halo_ref, near_ref, far_ref), out_ref.shape[0], store)


def log_pair_kernel(place_ref, axial_ref, halo_ref, near_ref, far_ref, scale_ref, first_ref, out_ref):
    def store(q, z, product):
        out_ref[q, 0, z] = first_ref[q, z]
        out_ref[q, 1, z] = jnp.log(product * scale_ref[q, z])

    depth_adjoint(place_ref, axial_ref, (halo_ref, near_ref, far_ref), out_ref.shape[0], store)


def share_kernel(place_ref, own_ref, copies_ref, current_ref):
    for k in range(2):
        at = place_ref[0] if k == 0 else 1 - place_ref[0]
        values = own_ref[at]
        current_ref[k] = values
        for q in range(copies_ref.shape[0]):
            copies_ref[q, k] = values


def corrected(pieces_ref, current_ref, k, views_total):
    total = pieces_ref[0, k]
    for q in range(1, pieces_ref.shape[0]):
        total = total + pieces_ref[q, k]
    return current_ref[k] * jnp.exp(total * (1.0 / views_total))


ANY = pl.BlockSpec(memory_space=pl.ANY)
SMEM = pl.BlockSpec(memory_space=pltpu.SMEM)
VMEM = pl.BlockSpec(memory_space=pltpu.VMEM)


def vmem(values):
    return pltpu.with_memory_space_constraint(values, pltpu.VMEM)


def hbm(values):
    return pltpu.with_memory_space_constraint(values, pltpu.HBM)


def call(kernel, in_specs, out_shape, out_specs, scratch=(), limit=10, **more):
    return pl.pallas_call(
        kernel,
        out_shape=out_shape,
        in_specs=in_specs,
        out_specs=out_specs,
        scratch_shapes=list(scratch),
        compiler_params=pltpu.CompilerParams(vmem_limit_bytes=limit * 1024 * 1024),
        cost_estimate=pl.CostEstimate(flops=1024, bytes_accessed=1024, transcendentals=0),
        **more,
    )


def body(estimate, observed, voxel_weights, lateral_taps, axial_taps):
    views, planes, height, breadth = observed.shape
    bases = voxel_weights.shape[1]
    half = planes // 2
    assert half == RADIUS and planes % 2 == 0
    quarters = lax.axis_size("view")
    depths = lax.axis_size("depth")
    span = height // quarters
    views_total = views * quarters
    voxel_total = planes * depths * height * breadth
    parity = lax.rem(lax.axis_index("depth"), 2).astype(jnp.int32)
    first_view, first_plane = lax.axis_index("view") * views, lax.axis_index("depth") * planes
    halves = [
        jnp.stack([at, first_view, first_plane + at * half]).astype(jnp.int32) for at in (parity, 1 - parity)
    ]

    def swap(values, which):
        pairs = []
        for i in range(1 - which, depths - 1, 2):
            pairs += [(i, i + 1), (i + 1, i)]
        return lax.ppermute(values, "depth", pairs)

    def shape(*dims, dtype=F32):
        return jax.ShapeDtypeStruct(dims, dtype)

    x_shape = shape(views, bases, breadth, breadth, dtype=BF16)
    y_shape = shape(views, bases * height, height, dtype=BF16)
    gain_shape = shape(views, bases, breadth)
    yt_shape = shape(views, height, bases * height, dtype=BF16)
    noise_shape = shape(noise_rows(bases, height), breadth)
    group_shape = shape(quarters, half, span, breadth)
    field_shape = shape(views, half, height, breadth)
    fidelity_shape = shape(views, 8, breadth)
    pair_shape = shape(quarters, 2, half, span, breadth)

    built = tuple(
        space(a.shape, a.dtype)
        for space, a in ((pltpu.HBM, x_shape), (pltpu.VMEM, x_shape), (pltpu.HBM, y_shape), (pltpu.VMEM, yt_shape),
                         (pltpu.HBM, noise_shape), (pltpu.VMEM, gain_shape)))
    *mats, axial = call(
        prepare_kernel, [SMEM, VMEM, VMEM], built + (shape(*axial_taps.shape),), (VMEM,) * 7,
    )(lateral_taps, lateral_taps, axial_taps)
    x_mat, y_mat, noise = (hbm(mats[k]) for k in (0, 2, 4))
    xt_mat, yt_mat, gain = (vmem(mats[k]) for k in (1, 3, 5))
    weights, counts = hbm(voxel_weights), hbm(observed)
    weights_buf = pltpu.VMEM((views, bases, half, height, breadth), BF16)
    counts_buf = pltpu.VMEM((views, half, height, breadth), F32)
    mixed_buf = pltpu.VMEM((views, half, 2 * bases * height, breadth), BF16)

    def ones(after):
        both_buf = pltpu.VMEM((2, views, bases, half, height, breadth), BF16)
        return call(
            ones_kernel, [SMEM, ANY, VMEM, VMEM, ANY], (field_shape, field_shape, shape(8, 128)), (VMEM,) * 3,
            [both_buf, mixed_buf, pltpu.SemaphoreType.DMA((2, views))], limit=22,
        )(jnp.stack(halves), weights, xt_mat, yt_mat, after)

    def step_half(which, halo, near, far, after, last):
        out = call(
            step_kernel if last else plain_step_kernel, [SMEM] * 2 + [VMEM] * 4 + [ANY] * 5 + [VMEM] * 2 + [ANY],
            (field_shape, fidelity_shape) if last else field_shape, (VMEM, VMEM) if last else VMEM,
            [pltpu.VMEM((views, half, 2 * height, breadth), BF16),
             pltpu.VMEM((views, bases, half * height, breadth), BF16), mixed_buf,
             weights_buf, counts_buf, pltpu.VMEM(noise_shape.shape, F32), pltpu.VMEM(y_shape.shape, BF16),
             pltpu.VMEM(x_shape.shape, BF16), pltpu.SemaphoreType.DMA((2, views)), pltpu.SemaphoreType.DMA((2 + views,))],
            limit=30,
        )(halves[which], axial, halo, near, far, gain, noise, y_mat, counts, weights, x_mat, xt_mat, yt_mat, after)
        return out if last else (out, None)

    def scale_half(which, halo, near, far, after):
        return call(scale_kernel, [SMEM] * 2 + [VMEM] * 3 + [ANY], group_shape, VMEM)(
            halves[which], axial, halo, near, far, after)

    def log_half(which, halo, near, far, scale, first):
        if first is None:
            return call(log_kernel, [SMEM] * 2 + [VMEM] * 4, group_shape, VMEM)(halves[which], axial, halo, near, far, scale)
        return call(log_pair_kernel, [SMEM] * 2 + [VMEM] * 5, pltpu.HBM(pair_shape.shape, F32), VMEM)(
            halves[which], axial, halo, near, far, scale, first)

    def share():
        own = estimate.reshape(2, half, span, breadth)
        return call(
            share_kernel, [SMEM, VMEM], (pltpu.HBM(pair_shape.shape, F32), pltpu.HBM(own.shape, F32)), (VMEM, VMEM))(
            halves[0], hbm(own))

    def update(pieces, current):
        def kernel(pieces_ref, current_ref, copies_ref, new_ref):
            for k in range(2):
                new_ref[k] = corrected(pieces_ref, current_ref, k, views_total)
                for q in range(quarters):
                    copies_ref[q, k] = new_ref[k]

        out_shape = (pltpu.HBM(pair_shape.shape, F32), pltpu.HBM(current.shape, F32))
        return call(kernel, [VMEM, VMEM], out_shape, (VMEM,) * 2)(pieces, hbm(current))

    def finish(pieces, current):
        def kernel(place_ref, pieces_ref, current_ref, out_ref):
            for k in range(2):
                at = place_ref[0] if k == 0 else 1 - place_ref[0]
                out_ref[at] = corrected(pieces_ref, current_ref, k, views_total)

        return call(kernel, [SMEM, VMEM, VMEM], shape(*current.shape), VMEM)(halves[0], pieces, hbm(current))

    def exchange(values):
        return lax.all_to_all(values, "view", 0, 0)

    copies, current = share()
    gathered = exchange(copies)
    *sens, token = ones(hbm(copies))
    zero = token[0, 0]
    groups = [gathered[:, k] + zero for k in range(2)]
    sens_halo = [swap(sens[k], k) for k in range(2)]
    scales = [None, None]
    for iteration in range(ITERS):
        last = iteration == ITERS - 1
        halo = [swap(groups[k], k) for k in range(2)]
        fields, parts, fields_halo = [None, None], [None, None], [None, None]
        for k in range(2):
            fields[k], parts[k] = step_half(k, halo[k], groups[k], groups[1 - k], fields[0] if k else axial, last)
            fields_halo[k] = swap(fields[k], k)
        if iteration == 0:
            for k in range(2):
                scales[k] = scale_half(k, sens_halo[k], sens[k], sens[1 - k], axial)
        logs = None
        for k in range(2):
            logs = log_half(k, fields_halo[k], fields[k], fields[1 - k], scales[k], logs)
        pieces = exchange(logs)
        if not last:
            copies, current = update(pieces, current)
            gathered = exchange(copies)
            groups = [gathered[:, k] for k in range(2)]
    divergence = lax.psum(jnp.sum(parts[0] + parts[1], axis=(1, 2)), "depth") / voxel_total
    updated = finish(pieces, current)
    return updated.reshape(estimate.shape), divergence


def solution(mesh):
    placed = (
        P("depth", "view", None),
        P("view", "depth", None, None),
        P("view", None, "depth", None, None),
        P("view", None, None, None),
        P("view", None),
    )
    return jax.shard_map(
        body,
        mesh=mesh,
        in_specs=placed,
        out_specs=(P("depth", "view", None), P("view")),
        check_vma=False,
    )
```

```python
import jax
import jax.numpy as jnp
from jax import lax
from jax.experimental import pallas as pl
from jax.experimental.pallas import tpu as pltpu
from jax.sharding import PartitionSpec as P

TAPS = 9
RADIUS = 4
ITERS = 2
F32 = jnp.float32
BF16 = jnp.bfloat16
NOISE_SHIFTS = 64


def mxu(left, right):
    return jnp.dot(left, right, preferred_element_type=F32)


def noise_rows(bases, height):
    return bases * height + 8 * NOISE_SHIFTS


def noise_at(place_ref, view, z, rows):
    shift = lax.rem(37 * (place_ref[1] + view) + 11 * (place_ref[2] + z), NOISE_SHIFTS)
    return pl.ds(pl.multiple_of(shift * 8, 8), rows)


def prepare_kernel(taps_ref, lateral_ref, axial_ref, x_ref, xt_ref, y_ref, yt_ref, noise_ref, gain_ref, axial_out_ref):
    prepare_noise(axial_ref, noise_ref, axial_out_ref)

    def each(view, carry):
        prepare_view(view, taps_ref, *(ref.at[view] for ref in (lateral_ref, x_ref, xt_ref, y_ref, yt_ref, gain_ref)))
        return carry

    lax.fori_loop(0, x_ref.shape[0], each, 0)


def prepare_view(view, taps_ref, lateral_ref, x_ref, xt_ref, y_ref, yt_ref, gain_ref):
    bases, breadth, height = x_ref.shape[0], x_ref.shape[1], yt_ref.shape[0]
    tall, wide = 32, 128
    inverses = []
    for base in range(bases):
        taps = lateral_ref[base]
        inverse = 1.0 / jnp.sum(taps, axis=-1, keepdims=True)
        sums = jnp.sum((taps * inverse).astype(BF16).astype(F32), axis=-1, keepdims=True)
        gain = 1.0 / (sums[0:1] * sums[1:2])
        gain_ref[base : base + 1, :] = jnp.broadcast_to(gain, (1, gain_ref.shape[1]))
        inverses.append([jnp.broadcast_to(inverse[k : k + 1], (tall, wide)) for k in range(2)])

    def banded(masks, base, kind):
        forward = turned = jnp.zeros((tall, wide), F32)
        for tap in range(TAPS):
            value = taps_ref[view, base, kind, tap]
            forward = jnp.where(masks[tap], value, forward)
            turned = jnp.where(masks[TAPS - 1 - tap], value, turned)
        return (forward * inverses[base][kind]).astype(BF16), (turned * inverses[base][kind]).astype(BF16)

    for r in range(0, breadth, tall):
        for c in range(0, breadth, wide):
            at = (slice(r, r + tall), slice(c, c + wide))
            lateral = r < height and c < height
            if r + tall + RADIUS <= c or c + wide + RADIUS <= r:
                empty = jnp.zeros((tall, wide), BF16)
                for base in range(bases):
                    x_ref[(base,) + at] = empty
                    xt_ref[(base,) + at] = empty
                    if lateral:
                        y_ref[base * height + r : base * height + r + tall, at[1]] = empty
                        yt_ref[at[0], base * height + c : base * height + c + wide] = empty
                continue
            rows = lax.broadcasted_iota(jnp.int32, (tall, wide), 0) + r
            columns = lax.broadcasted_iota(jnp.int32, (tall, wide), 1) + c
            masks = [rows - columns + RADIUS == tap for tap in range(TAPS)]
            for base in range(bases):
                forward, turned = banded(masks, base, 1)
                x_ref[(base,) + at] = forward
                xt_ref[(base,) + at] = turned
                if lateral:
                    forward, turned = banded(masks, base, 0)
                    y_ref[base * height + r : base * height + r + tall, at[1]] = turned
                    yt_ref[at[0], base * height + c : base * height + c + wide] = forward


def prepare_noise(axial_ref, noise_ref, axial_out_ref):
    axial = axial_ref[...]
    axial_out_ref[...] = axial / jnp.sum(axial, axis=-1, keepdims=True)

    def fill(k, carry):
        first = pl.multiple_of(k * 64, 64)
        rows = lax.broadcasted_iota(jnp.int32, (64, noise_ref.shape[1]), 0) + first
        columns = lax.broadcasted_iota(jnp.int32, (64, noise_ref.shape[1]), 1)
        mixed = rows * 1664525 + columns * 22695477 + 12345
        for odd, shift in ((739982445, 15), (695872825, 12)):
            mixed = (mixed ^ lax.shift_right_logical(mixed, shift)) * odd
        mixed = mixed ^ lax.shift_right_logical(mixed, 15)
        both = (mixed & 2047) + (lax.shift_right_logical(mixed, 16) & 2047)
        noise_ref[pl.ds(first, 64), :] = 1.0 + (both - 2047).astype(F32) * (1.0 / (2048 * 128))
        return carry

    lax.fori_loop(0, noise_ref.shape[0] // 64, fill, 0)


def adjoint_base(values, base, xt, mixed):
    half, rows, _ = mixed.shape
    height = values.shape[0] // half
    swept = mxu(values, xt[base])
    high = swept.astype(BF16)
    low = (swept - high.astype(F32)).astype(BF16)
    for z in range(half):
        at = slice(z * height, (z + 1) * height)
        mixed[z, base * height : (base + 1) * height, :] = high[at]
        mixed[z, rows // 2 + base * height : rows // 2 + (base + 1) * height, :] = low[at]


def adjoint_rows(yt, mixed, z):
    return mxu(jnp.concatenate([yt[...], yt[...]], axis=1), mixed[z])


def fetch(place_ref, source_any, buffer, sems):
    half = buffer.shape[-3]
    planes = pl.ds(place_ref[0] * half, half)
    copies = []
    for view in range(buffer.shape[0]):
        source = source_any.at[view, planes] if len(buffer.shape) == 4 else source_any.at[view, :, planes]
        copies.append(pltpu.make_async_copy(source, buffer.at[view], sems.at[view]))
        copies[-1].start()
    return copies


def ones_kernel(places_ref, weights_any, xt, yt, after_any, first_ref, second_ref, token_ref, weights, mixed, sems):
    views, half, height, breadth = first_ref.shape
    fields = (first_ref, second_ref)
    copies = [fetch(places_ref.at[k], weights_any, weights.at[k], sems.at[k]) for k in range(2)]
    token_ref[...] = jnp.zeros(token_ref.shape, F32)
    for k, field_ref in enumerate(fields):
        for view in range(views):
            copies[k][view].wait()
            for base in range(weights.shape[2]):
                values = weights[k, view, base].reshape(half * height, breadth)
                adjoint_base(values, base, xt.at[view], mixed.at[view])
            for z in range(half):
                field_ref[view, z] = adjoint_rows(yt.at[view], mixed.at[view], z)


def step_kernel(place_ref, axial_ref, halo_ref, near_ref, far_ref, gain_ref, noise_any, y_any, counts_any, weights_any,
                x_any, xt, yt, after_any, field_ref, fidelity_ref, blurred, rows, mixed, weights, counts, noise_ref, y, x,
                sems, more_sems):
    views, half, height, breadth = field_ref.shape
    bases = weights.shape[1]
    quarters, _, span, _ = near_ref.shape
    early = [pltpu.make_async_copy(noise_any, noise_ref, more_sems.at[0]), pltpu.make_async_copy(y_any, y, more_sems.at[1])]
    for copy in early:
        copy.start()
    x_copies = [pltpu.make_async_copy(x_any.at[v], x.at[v], more_sems.at[2 + v]) for v in range(views)]
    for copy in x_copies:
        copy.start()
    weights_copies = fetch(place_ref, weights_any, weights, sems.at[0])
    counts_copies = fetch(place_ref, counts_any, counts, sems.at[1])

    def depth_blur(groups):
        for view in range(views):
            for z in range(half):
                for q in range(quarters):
                    total = None
                    for tap in range(TAPS):
                        plane = z + tap
                        term = axial_ref[view, tap] * groups[plane // half][q, plane % half]
                        total = term if total is None else total + term
                    high = total.astype(BF16)
                    blurred[view, z, q * span : (q + 1) * span, :] = high
                    low = (total - high.astype(F32)).astype(BF16)
                    blurred[view, z, height + q * span : height + (q + 1) * span, :] = low

    @pl.when(place_ref[0] == 0)
    def _():
        depth_blur((halo_ref, near_ref, far_ref))

    @pl.when(place_ref[0] != 0)
    def _():
        depth_blur((far_ref, near_ref, halo_ref))

    def sweep_rows(view, z):
        twice = jnp.concatenate([y[view], y[view]], axis=1)
        swept = mxu(twice, blurred[view, z]) * noise_ref[noise_at(place_ref, view, z, bases * height), :]
        for base in range(bases):
            gain = gain_ref[view, base : base + 1, :]
            part = (swept[base * height : (base + 1) * height] * gain).astype(BF16)
            rows[view, base, z * height : (z + 1) * height, :] = part

    def weights_of(view, base):
        return weights[view, base].reshape(half * height, breadth).astype(F32)

    predicted, spread = [None] * views, [None] * views

    def predict(view, base):
        term = weights_of(view, base) * mxu(rows[view, base], x[view, base])
        predicted[view] = term if base == 0 else predicted[view] + term

    def compare(view):
        observed = counts[view].reshape(half * height, breadth)
        ratios = observed / predicted[view]
        if fidelity_ref is not None:
            terms = observed * jnp.log(ratios) - observed + predicted[view]
            fidelity_ref[view] = jnp.sum(terms.reshape(-1, 8, breadth), axis=0)
        noise = [noise_ref[noise_at(place_ref, view, z, height), :] for z in range(half)]
        spread[view] = ratios * jnp.concatenate(noise, axis=0)

    def back(view, base):
        adjoint_base((weights_of(view, base) * spread[view]).astype(BF16), base, xt.at[view], mixed.at[view])

    def back_rows(view, z):
        field_ref[view, z] = adjoint_rows(yt.at[view], mixed.at[view], z)

    for copy in early:
        copy.wait()
    for z in range(half):
        sweep_rows(0, z)
    for view in range(views):
        following = view + 1 < views
        x_copies[view].wait()
        weights_copies[view].wait()
        counts_copies[view].wait()
        for base in range(bases):
            predict(view, base)
            if following and (base + 1) % (bases // half) == 0:
                sweep_rows(view + 1, base // (bases // half))
            if view > 0:
                back(view - 1, base)
        compare(view)
        if view > 0:
            for z in range(half):
                back_rows(view - 1, z)
    for base in range(bases):
        back(views - 1, base)
    for z in range(half):
        back_rows(views - 1, z)


def plain_step_kernel(*refs):
    step_kernel(*refs[:15], None, *refs[15:])


def depth_adjoint(place_ref, axial_ref, groups, quarters, write):
    views, half, height, _ = groups[1].shape
    span = height // quarters

    def run(ordered):
        def quarter(q, carry):
            at = pl.ds(pl.multiple_of(q * span, span), span)
            for z in range(half):
                product = None
                for view in range(views):
                    total = None
                    for tap in range(TAPS):
                        plane = z + 2 * RADIUS - tap
                        term = axial_ref[view, tap] * ordered[plane // half][view, plane % half, at, :]
                        total = term if total is None else total + term
                    product = total if product is None else product * total
                write(q, z, product)
            return carry

        lax.fori_loop(0, quarters, quarter, 0)

    halo_ref, near_ref, far_ref = groups

    @pl.when(place_ref[0] == 0)
    def _():
        run((halo_ref, near_ref, far_ref))

    @pl.when(place_ref[0] != 0)
    def _():
        run((far_ref, near_ref, halo_ref))


def scale_kernel(place_ref, axial_ref, halo_ref, near_ref, far_ref, after_any, out_ref):
    def store(q, z, product):
        out_ref[q, z] = 1.0 / product

    depth_adjoint(place_ref, axial_ref, (halo_ref, near_ref, far_ref), out_ref.shape[0], store)


def log_kernel(place_ref, axial_ref, halo_ref, near_ref, far_ref, scale_ref, out_ref):
    def store(q, z, product):
        out_ref[q, z] = jnp.log(product * scale_ref[q, z])

    depth_adjoint(place_ref, axial_ref, (halo_ref, near_ref, far_ref), out_ref.shape[0], store)


def log_pair_kernel(place_ref, axial_ref, halo_ref, near_ref, far_ref, scale_ref, first_ref, out_ref):
    def store(q, z, product):
        out_ref[q, 0, z] = first_ref[q, z]
        out_ref[q, 1, z] = jnp.log(product * scale_ref[q, z])

    depth_adjoint(place_ref, axial_ref, (halo_ref, near_ref, far_ref), out_ref.shape[0], store)


def share_kernel(place_ref, own_ref, copies_ref, current_ref):
    for k in range(2):
        at = place_ref[0] if k == 0 else 1 - place_ref[0]
        values = own_ref[at]
        current_ref[k] = values
        for q in range(copies_ref.shape[0]):
            copies_ref[q, k] = values


def corrected(pieces_ref, current_ref, k, views_total):
    total = pieces_ref[0, k]
    for q in range(1, pieces_ref.shape[0]):
        total = total + pieces_ref[q, k]
    return current_ref[k] * jnp.exp(total * (1.0 / views_total))


ANY = pl.BlockSpec(memory_space=pl.ANY)
SMEM = pl.BlockSpec(memory_space=pltpu.SMEM)
VMEM = pl.BlockSpec(memory_space=pltpu.VMEM)


def vmem(values):
    return pltpu.with_memory_space_constraint(values, pltpu.VMEM)


def hbm(values):
    return pltpu.with_memory_space_constraint(values, pltpu.HBM)


def call(kernel, in_specs, out_shape, out_specs, scratch=(), limit=10, **more):
    return pl.pallas_call(
        kernel,
        out_shape=out_shape,
        in_specs=in_specs,
        out_specs=out_specs,
        scratch_shapes=list(scratch),
        compiler_params=pltpu.CompilerParams(vmem_limit_bytes=limit * 1024 * 1024),
        cost_estimate=pl.CostEstimate(flops=1024, bytes_accessed=1024, transcendentals=0),
        **more,
    )


def body(estimate, observed, voxel_weights, lateral_taps, axial_taps):
    views, planes, height, breadth = observed.shape
    bases = voxel_weights.shape[1]
    half = planes // 2
    assert half == RADIUS and planes % 2 == 0
    quarters = lax.axis_size("view")
    depths = lax.axis_size("depth")
    span = height // quarters
    views_total = views * quarters
    voxel_total = planes * depths * height * breadth
    parity = lax.rem(lax.axis_index("depth"), 2).astype(jnp.int32)
    first_view, first_plane = lax.axis_index("view") * views, lax.axis_index("depth") * planes
    halves = [
        jnp.stack([at, first_view, first_plane + at * half]).astype(jnp.int32) for at in (parity, 1 - parity)
    ]

    def swap(values, which):
        pairs = []
        for i in range(1 - which, depths - 1, 2):
            pairs += [(i, i + 1), (i + 1, i)]
        return lax.ppermute(values, "depth", pairs)

    def shape(*dims, dtype=F32):
        return jax.ShapeDtypeStruct(dims, dtype)

    x_shape = shape(views, bases, breadth, breadth, dtype=BF16)
    y_shape = shape(views, bases * height, height, dtype=BF16)
    gain_shape = shape(views, bases, breadth)
    yt_shape = shape(views, height, bases * height, dtype=BF16)
    noise_shape = shape(noise_rows(bases, height), breadth)
    group_shape = shape(quarters, half, span, breadth)
    field_shape = shape(views, half, height, breadth)
    fidelity_shape = shape(views, 8, breadth)
    pair_shape = shape(quarters, 2, half, span, breadth)

    built = tuple(
        space(a.shape, a.dtype)
        for space, a in ((pltpu.HBM, x_shape), (pltpu.VMEM, x_shape), (pltpu.HBM, y_shape), (pltpu.VMEM, yt_shape),
                         (pltpu.HBM, noise_shape), (pltpu.VMEM, gain_shape)))
    *mats, axial = call(
        prepare_kernel, [SMEM, VMEM, VMEM], built + (shape(*axial_taps.shape),), (VMEM,) * 7,
    )(lateral_taps, lateral_taps, axial_taps)
    x_mat, y_mat, noise = (hbm(mats[k]) for k in (0, 2, 4))
    xt_mat, yt_mat, gain = (vmem(mats[k]) for k in (1, 3, 5))
    weights, counts = hbm(voxel_weights), hbm(observed)
    weights_buf = pltpu.VMEM((views, bases, half, height, breadth), BF16)
    counts_buf = pltpu.VMEM((views, half, height, breadth), F32)
    mixed_buf = pltpu.VMEM((views, half, 2 * bases * height, breadth), BF16)

    def ones(after):
        both_buf = pltpu.VMEM((2, views, bases, half, height, breadth), BF16)
        return call(
            ones_kernel, [SMEM, ANY, VMEM, VMEM, ANY],
            (pltpu.HBM(field_shape.shape, F32), pltpu.HBM(field_shape.shape, F32), shape(8, 128)), (VMEM,) * 3,
            [both_buf, mixed_buf, pltpu.SemaphoreType.DMA((2, views))], limit=22,
        )(jnp.stack(halves), weights, xt_mat, yt_mat, after)

    def step_half(which, halo, near, far, after, last):
        out = call(
            step_kernel if last else plain_step_kernel, [SMEM] * 2 + [VMEM] * 4 + [ANY] * 5 + [VMEM] * 2 + [ANY],
            (field_shape, fidelity_shape) if last else field_shape, (VMEM, VMEM) if last else VMEM,
            [pltpu.VMEM((views, half, 2 * height, breadth), BF16),
             pltpu.VMEM((views, bases, half * height, breadth), BF16), mixed_buf,
             weights_buf, counts_buf, pltpu.VMEM(noise_shape.shape, F32), pltpu.VMEM(y_shape.shape, BF16),
             pltpu.VMEM(x_shape.shape, BF16), pltpu.SemaphoreType.DMA((2, views)), pltpu.SemaphoreType.DMA((2 + views,))],
            limit=30,
        )(halves[which], axial, halo, near, far, gain, noise, y_mat, counts, weights, x_mat, xt_mat, yt_mat, after)
        return out if last else (out, None)

    def scale_half(which, halo, near, far, after):
        return call(scale_kernel, [SMEM] * 2 + [VMEM] * 3 + [ANY], group_shape, VMEM)(
            halves[which], axial, halo, hbm(near), hbm(far), after)

    def log_half(which, halo, near, far, scale, first):
        if first is None:
            return call(log_kernel, [SMEM] * 2 + [VMEM] * 4, group_shape, VMEM)(halves[which], axial, halo, near, far, scale)
        return call(log_pair_kernel, [SMEM] * 2 + [VMEM] * 5, pltpu.HBM(pair_shape.shape, F32), VMEM)(
            halves[which], axial, halo, near, far, scale, first)

    def share():
        own = estimate.reshape(2, half, span, breadth)
        return call(
            share_kernel, [SMEM, VMEM], (pltpu.HBM(pair_shape.shape, F32), pltpu.HBM(own.shape, F32)), (VMEM, VMEM))(
            halves[0], hbm(own))

    def part(pair, after):
        def kernel(pair_ref, after_any, *out_refs):
            for k in range(2):
                out_refs[k][...] = pair_ref[:, k]

        return call(kernel, [VMEM, ANY], (pltpu.VMEM(group_shape.shape, F32),) * 2, (VMEM, VMEM))(vmem(pair), after)

    def update(pieces, current):
        def kernel(pieces_ref, current_ref, copies_ref, new_ref):
            for k in range(2):
                new_ref[k] = corrected(pieces_ref, current_ref, k, views_total)
                for q in range(quarters):
                    copies_ref[q, k] = new_ref[k]

        out_shape = (pltpu.HBM(pair_shape.shape, F32), pltpu.HBM(current.shape, F32))
        return call(kernel, [VMEM, VMEM], out_shape, (VMEM,) * 2)(pieces, hbm(current))

    def finish(pieces, current):
        def kernel(place_ref, pieces_ref, current_ref, out_ref):
            for k in range(2):
                at = place_ref[0] if k == 0 else 1 - place_ref[0]
                out_ref[at] = corrected(pieces_ref, current_ref, k, views_total)

        return call(kernel, [SMEM, VMEM, VMEM], shape(*current.shape), VMEM)(halves[0], pieces, hbm(current))

    def exchange(values):
        return lax.all_to_all(values, "view", 0, 0)

    copies, current = share()
    gathered = exchange(copies)
    *sens, token = ones(hbm(copies))
    groups = part(gathered, token)
    sens_halo = [swap(sens[k], k) for k in range(2)]
    scales = [None, None]
    for iteration in range(ITERS):
        last = iteration == ITERS - 1
        halo = [swap(groups[k], k) for k in range(2)]
        fields, parts, fields_halo = [None, None], [None, None], [None, None]
        for k in range(2):
            fields[k], parts[k] = step_half(k, halo[k], groups[k], groups[1 - k], fields[0] if k else axial, last)
            fields_halo[k] = swap(fields[k], k)
        if iteration == 0:
            for k in range(2):
                scales[k] = scale_half(k, sens_halo[k], sens[k], sens[1 - k], axial)
        logs = None
        for k in range(2):
            logs = log_half(k, fields_halo[k], fields[k], fields[1 - k], scales[k], logs)
        pieces = exchange(logs)
        if not last:
            copies, current = update(pieces, current)
            gathered = exchange(copies)
            groups = [gathered[:, k] for k in range(2)]
    divergence = lax.psum(jnp.sum(parts[0] + parts[1], axis=(1, 2)), "depth") / voxel_total
    updated = finish(pieces, current)
    return updated.reshape(estimate.shape), divergence


def solution(mesh):
    placed = (
        P("depth", "view", None),
        P("view", "depth", None, None),
        P("view", None, "depth", None, None),
        P("view", None, None, None),
        P("view", None),
    )
    return jax.shard_map(
        body,
        mesh=mesh,
        in_specs=placed,
        out_specs=(P("depth", "view", None), P("view")),
        check_vma=False,
    )
```
